32 devices in a mesh: groups: 2 (over x), space: 16 (over z, y, core).
Axes of the slice: x: 2, y: 2, z: 4, core: 2. Of those that a mesh axis runs over, the one named last changes fastest.
Arguments:
- slowness: float32 [512, 4096], P(('groups', 'space')), parts along dimension 0, may hold values from 0.25 to 1
- ocean: int32 [512, 4096], P(('groups', 'space')), parts along dimension 0, may hold values 0 or 1
- start_times: float32 [8, 256, 4096], P('groups', 'space'), parts along dimension 0, may hold values from 0 to 96
- source_cells: int32 [8], P('groups'), parts along dimension 0, may hold values from 0 to 1048575
- gauge_cells: int32 [4096], P(('groups', 'space')), parts along dimension 0, may hold values from 0 to 65535
- gauge_owner: int32 [4096, 1], P(('groups', 'space')), parts along dimension 0, may hold values from 0 to 15; in each aligned block of 128 rows (0 to 127, 128 to 255, ...) at most 16 rows name the same one
Outputs:
- arrival: float32 [512, 4096], P(('groups', 'space')), parts along dimension 0
- gauge_arrivals: float32 [32, 4, 256], P(('groups', 'space')), parts along dimension 0
The draws below stay inside these ranges and needn't reach their ends.
There are 2 independent parts, one for each index of `groups`. The reference program is written for one: setup_inputs(seed, part) draws one part's arguments, and reference() takes and returns one part's arrays. A program takes and returns all parts, laid end to end along the dimension named above; each array names one. Nothing has to cross between parts.
Inputs may be any that keep to these rules, and one draw needn't show every extreme that they name: `gauge_owner`: among the 128 gauges of one device block, no owner is named more than 16 times, a bound that some block reaches.
All inputs are finite; a program needn't handle non-finite values. No bound on the sum of `ocean` on one device may be relied on, other than what follows from the above.
Results may differ from the reference program's by a relative error of at most 0.00016.
Values sent between devices are 32-bit elements; how exact they have to be, the bound alone decides.
A program may use at most 128 MiB of HBM per device.

```python
import math
import jax
import jax.numpy as jnp
import numpy as np
from jax import lax

R_DEV = 16
W = 4096
SOURCES = 4
SWEEPS = 8
BLOCKS = 3
G_DEV = 128
NROWS = 256
GAUGES = 2048
CAP = 16
N_SPACE = 16


def draw_start_times(key, part):
    key_list = jax.random.split(jax.random.fold_in(key, 7), 7)
    sweep_total = BLOCKS * SWEEPS
    row_frac = jnp.arange(NROWS, dtype=jnp.float32)[None, :, None] / NROWS
    col_frac = jnp.arange(W, dtype=jnp.float32)[None, None, :] / W
    wave_rows = jax.random.randint(key_list[0], (SOURCES, 1, 1), 1, 5).astype(jnp.float32)
    wave_cols = jax.random.randint(key_list[1], (SOURCES, 1, 1), 1, 5).astype(jnp.float32)
    phase_rows = jax.random.uniform(key_list[2], (SOURCES, 1, 1), jnp.float32)
    phase_cols = jax.random.uniform(key_list[3], (SOURCES, 1, 1), jnp.float32)
    smooth = 0.5 + 0.5 * jnp.sin(2.0 * math.pi * (wave_rows * row_frac + phase_rows)) * jnp.cos(2.0 * math.pi * (wave_cols * col_frac + phase_cols))
    grid_shape = (SOURCES, NROWS, W)
    rough_part = jax.random.uniform(key_list[4], grid_shape, jnp.float32)
    seeded = jax.random.randint(key_list[5], grid_shape, 0, 4 * sweep_total * sweep_total) == 0
    seed_value = jax.random.uniform(key_list[6], grid_shape, jnp.float32)
    ceiling = 20.0 + 50.0 * smooth + 6.0 * rough_part
    lowest = 6.0 * seed_value
    return jnp.where(seeded, lowest, ceiling).astype(jnp.float32)


def set_ends(entries, rng, least, largest):
    longest = entries.shape.index(max(entries.shape))
    spots = []
    for shift in (0, 1):
        where = [jax.random.randint(jax.random.fold_in(rng, axis), (), 0, length) for axis, length in enumerate(entries.shape)]
        where[longest] = (where[longest] + shift) % entries.shape[longest]
        spots.append(tuple(where))
    return entries.at[spots[0]].set(least).at[spots[1]].set(largest)


def block_levels(rng, dims, cuts, least, high):
    def one(dim, shards_of):
        steps = jax.random.uniform(jax.random.fold_in(jax.random.fold_in(rng, 6), dim), (shards_of,), jnp.float32, least / len(cuts), high / len(cuts))
        return jnp.repeat(jnp.exp(steps), dims[dim] // shards_of).reshape((-1,) + (1,) * (len(dims) - dim - 1))

    loudness = one(*cuts[0])
    for cut in cuts[1:]:
        loudness = loudness * one(*cut)
    return loudness


def routed_block(key, own, number, rows, count, top, most, lean):
    sequence = jax.random.permutation(key, count)
    crowded, usual = load_shares(count, rows * top, most, lean, True), load_shares(count, rows * top, most, lean, False)
    places = jnp.arange(count)

    def named(sizes, offset_by):
        used = int((sizes > 0).sum())
        fixed = max(1, used // 4)
        moved = fixed + (places - fixed + offset_by * (used - fixed)) % max(1, count - fixed)
        return jnp.zeros((count,), jnp.int32).at[sequence[jnp.where(places < fixed, places, moved)]].set(jnp.asarray(sizes, jnp.int32))

    sizes = jnp.where(number % 4 == 0, named(crowded, number // 4), named(usual, number - number // 4 - 1))
    mixed = jax.random.permutation(jax.random.fold_in(own, 3), count)
    source_of, taker = mixed[0:count // 2 * 2:2], mixed[1:count // 2 * 2:2]
    room = jnp.minimum(sizes[source_of] - 1, most - sizes[taker]) // 2
    room = jnp.where((source_of == sequence[0]) | (taker == sequence[0]) | (sizes[taker] == 0), 0, jnp.maximum(room, 0))
    moved = jax.random.randint(jax.random.fold_in(own, 4), (count // 2,), 0, 1 << 20) % (room + 1)
    sizes = sizes.at[source_of].add(-moved).at[taker].add(moved)
    items = jnp.searchsorted(jnp.cumsum(sizes), jnp.arange(rows * top), side="right").astype(jnp.int32)
    listing = items.reshape(top, rows).T
    listing = listing[jax.random.permutation(jax.random.fold_in(own, 1), rows)]
    offset_by = jax.random.randint(jax.random.fold_in(own, 2), (rows, 1), 0, top)
    return jnp.take_along_axis(listing, (jnp.arange(top)[None, :] + offset_by) % top, axis=1)


def load_shares(amount, total, reach, slope, full):
    loads = [(1 << 20) // math.isqrt(grade ** slope) + 1 for grade in range(1, amount + 1)]
    largest = reach if full else min(reach, max(-(-total // amount), total * loads[0] // sum(loads)))
    least = 1 if total - largest >= amount - 1 else 0
    holding, rest = [largest] + [least] * (amount - 1), total - largest - least * (amount - 1)
    while rest > 0:
        movable = [i for i in range(1, amount) if holding[i] < largest] or [i for i in range(1, amount) if holding[i] < reach]
        pool, remaining = sum([loads[i] for i in movable]), rest
        for i in movable:
            addition = min(reach - holding[i], max(1, remaining * loads[i] // pool), rest)
            holding[i] = holding[i] + addition
            rest = rest - addition
    return np.array(holding)


def setup_inputs(seed: int = 0, part: int = 0) -> dict:
    seeds = jax.random.split(jax.random.key(seed), 7)
    part_splits = jax.random.split(jax.random.fold_in(seeds[6], part), 7)
    slowness = jnp.clip(jnp.exp(math.log(1.0) - 1.3862944 * jax.random.uniform(part_splits[0], (NROWS, W), jnp.float32) ** block_levels(part_splits[0], (NROWS, W), ((0, 16),), -0.2, 0.2)), 0.25, 1.0)
    ocean = set_ends((jax.random.randint(part_splits[1], (NROWS, W), 0, 10) < 9).astype(jnp.int32), jax.random.fold_in(part_splits[1], 1), 0, 1)
    start_times = draw_start_times(jax.random.fold_in(jax.random.fold_in(seeds[6], part), 71), part)
    source_cells = set_ends(jax.random.randint(part_splits[3], (SOURCES,), 0, NROWS * W), jax.random.fold_in(part_splits[3], 1), 0, (NROWS * W) - 1).astype(jnp.int32)
    gauge_cells = set_ends(jax.random.randint(part_splits[4], (GAUGES,), 0, R_DEV * W), jax.random.fold_in(part_splits[4], 1), 0, (R_DEV * W) - 1).astype(jnp.int32)
    gauge_owner_keys = jax.random.split(jax.random.fold_in(part_splits[5], 1), GAUGES // G_DEV)
    gauge_owner_turns = jax.random.permutation(jax.random.fold_in(part_splits[5], 3), GAUGES // G_DEV)
    gauge_owner = jax.vmap(lambda own, number: routed_block(jax.random.fold_in(part_splits[5], 2), own, number, G_DEV, N_SPACE, 1, CAP, 2))(gauge_owner_keys, gauge_owner_turns).reshape((GAUGES, 1))
    return {"slowness": slowness, "ocean": ocean, "start_times": start_times, "source_cells": source_cells, "gauge_cells": gauge_cells, "gauge_owner": gauge_owner}


far_value = 1.0e6
land_cost = 1.0e4
clip_value = 48.0
root_two = 1.41421356
root_five = 2.23606798


def relax(padded, cost):
    height = padded.shape[1] - 4
    width = padded.shape[2] - 4

    def shifted(drow, dcol):
        return padded[:, 2 + drow:2 + drow + height, 2 + dcol:2 + dcol + width]

    near = jnp.minimum(jnp.minimum(shifted(0, 1), shifted(0, -1)), jnp.minimum(shifted(1, 0), shifted(-1, 0)))
    diag = jnp.minimum(jnp.minimum(shifted(1, 1), shifted(1, -1)), jnp.minimum(shifted(-1, 1), shifted(-1, -1)))
    knight = jnp.minimum(jnp.minimum(shifted(1, 2), shifted(1, -2)), jnp.minimum(shifted(-1, 2), shifted(-1, -2)))
    knight = jnp.minimum(knight, jnp.minimum(jnp.minimum(shifted(2, 1), shifted(2, -1)), jnp.minimum(shifted(-2, 1), shifted(-2, -1))))
    best = jnp.minimum(near + cost, diag + root_two * cost)
    best = jnp.minimum(best, knight + root_five * cost)
    return jnp.minimum(shifted(0, 0), best)


def reference(slowness, ocean, start_times, source_cells, gauge_cells, gauge_owner):
    cost = jnp.where(ocean == 1, slowness, jnp.float32(land_cost))
    flat = jnp.arange(NROWS * W, dtype=jnp.int32).reshape(NROWS, W)
    seeded = jnp.where(flat[None] == source_cells[:, None, None], jnp.float32(0.0), start_times)

    def sweep(step, field):
        padded = jnp.pad(field, ((0, 0), (2, 2), (2, 2)), constant_values=far_value)
        return relax(padded, cost)

    def settle(field):
        return lax.fori_loop(0, BLOCKS * SWEEPS, sweep, field[None])[0]

    times = lax.map(settle, seeded)
    each_arrival = jnp.minimum(times, jnp.float32(clip_value)) / clip_value
    arrival = jnp.min(each_arrival, axis=0)
    blocks = each_arrival.reshape(SOURCES, N_SPACE, R_DEV * W)
    cells = gauge_cells.reshape(N_SPACE, G_DEV)
    values = jnp.take_along_axis(blocks, cells[None], axis=2)
    owners = gauge_owner.reshape(N_SPACE, G_DEV)
    onehot = (owners[:, :, None] == jnp.arange(N_SPACE, dtype=jnp.int32)[None, None, :]).astype(jnp.int32)
    ranks = jnp.sum((jnp.cumsum(onehot, axis=1) - 1) * onehot, axis=2)
    holder = jnp.arange(N_SPACE, dtype=jnp.int32)[:, None] * CAP + ranks
    result = jnp.zeros((N_SPACE, SOURCES, N_SPACE * CAP), jnp.float32)
    moved = jnp.transpose(values, (1, 2, 0)).reshape(N_SPACE * G_DEV, SOURCES)
    result = result.at[owners.reshape(-1), :, holder.reshape(-1)].set(moved)
    return arrival, result
```

```python
import functools

import jax
import jax.numpy as jnp
from jax import lax
from jax.experimental import pallas as pl
from jax.experimental.pallas import tpu as pltpu
from jax.sharding import PartitionSpec as P

SWEEPS = 8
BLOCKS = 3
HALO = 2 * SWEEPS

far_value = 1000000.0
land_cost = 10000.0
clip_value = 48.0
root_two = 1.41421356
root_five = 2.23606798

LANES = 128
SUBS = 8
VMEM = pl.BlockSpec(memory_space=pltpu.VMEM)
SMEM = pl.BlockSpec(memory_space=pltpu.SMEM)
PARAMS = pltpu.CompilerParams(vmem_limit_bytes=48 * 1024 * 1024)


def pack_rows(rows, phases, flat, turned, out_ref):
    @pl.loop(0, rows)
    def _(r):
        turned[...] = flat[pl.ds(pl.multiple_of(r * LANES, LANES), LANES), :].T
        for k in range(phases):
            out_ref[r, k] = turned[pl.ds(k, SUBS, stride=phases), :]


def prepare(first_ref, cells_ref, start_ref, cost_ref, times_ref, packed_ref, flat, turned):
    sources, rows, width = start_ref.shape
    tiles = width // LANES
    phases = LANES // SUBS
    high = cost_ref.shape[0]
    rowcol = lax.broadcasted_iota(jnp.int32, (rows, LANES), 0) * width + lax.broadcasted_iota(
        jnp.int32, (rows, LANES), 1
    )
    for s in range(sources):
        offset = cells_ref[s] - first_ref[0]
        for m in range(tiles):
            piece = start_ref[s, :, m * LANES : (m + 1) * LANES]
            piece = jnp.where(rowcol == offset - m * LANES, 0.0, piece)
            flat[pl.ds(s * tiles + m, rows, stride=LANES), :] = piece
    pack_rows(rows, phases, flat, turned, times_ref)
    for m in range(tiles):
        piece = cost_ref[:, m * LANES : (m + 1) * LANES]
        for s in range(sources):
            flat[pl.ds(s * tiles + m, high, stride=LANES), :] = piece
    pack_rows(high, phases, flat, turned, packed_ref)


def edge_fixers(tiles):
    sub = lax.broadcasted_iota(jnp.int32, (SUBS, LANES), 0)
    lane = lax.broadcasted_iota(jnp.int32, (SUBS, LANES), 1)
    first = lane % tiles == 0
    last = lane % tiles == tiles - 1
    far = jnp.float32(far_value)

    def from_left(x):
        y = pltpu.roll(x, 1, 0)
        z = jnp.where(first, far, pltpu.roll(y, 1, 1))
        return jnp.where(sub == 0, z, y)

    def from_right(x):
        y = pltpu.roll(x, SUBS - 1, 0)
        z = jnp.where(last, far, pltpu.roll(y, LANES - 1, 1))
        return jnp.where(sub == SUBS - 1, z, y)

    return from_left, from_right


def relax_block(tiles, fence_ref, prev_ref, cur_ref, next_ref, cost_ref, out_ref, one, two, cost2, cost5):
    rows, phases = cur_ref.shape[0], cur_ref.shape[1]
    high = cost_ref.shape[0]
    from_left, from_right = edge_fixers(tiles)

    def store_row(buf, r, vals):
        for k in range(phases):
            buf[r, 2 + k] = vals[k]
        buf[r, 0] = from_left(vals[phases - 2])
        buf[r, 1] = from_left(vals[phases - 1])
        buf[r, phases + 2] = from_right(vals[0])
        buf[r, phases + 3] = from_right(vals[1])

    @pl.loop(0, rows)
    def _(r):
        store_row(one, HALO + r, [cur_ref[r, k] for k in range(phases)])

    @pl.loop(0, HALO)
    def _(r):
        store_row(one, r, [jnp.maximum(prev_ref[r, k], fence_ref[0]) for k in range(phases)])
        store_row(
            one, HALO + rows + r, [jnp.maximum(next_ref[r, k], fence_ref[1]) for k in range(phases)]
        )

    @pl.loop(0, high)
    def _(r):
        for k in range(phases):
            c = cost_ref[r, k]
            cost2[r, k] = c * root_two
            cost5[r, k] = c * root_five

    def sweep(src, dst, lowest):
        count = (high - 2 * lowest) // 2

        @pl.loop(0, count)
        def _(pair):
            r0 = lowest + 2 * pair
            outs = ([], [])
            total = phases + 4
            t = [[src[r0 + d, k] for k in range(total)] for d in range(-2, 4)]
            for i in range(2):
                mid = t[2 + i]
                v1 = [jnp.minimum(t[1 + i][k], t[3 + i][k]) for k in range(total)]
                v2 = [
                    jnp.minimum(t[i][k], t[4 + i][k]) if 0 < k < total - 1 else None
                    for k in range(total)
                ]
                for k in range(2, phases + 2):
                    near = jnp.minimum(v1[k], jnp.minimum(mid[k - 1], mid[k + 1]))
                    diag = jnp.minimum(v1[k - 1], v1[k + 1])
                    knight = jnp.minimum(
                        jnp.minimum(v1[k - 2], v1[k + 2]), jnp.minimum(v2[k - 1], v2[k + 1])
                    )
                    best = jnp.minimum(
                        near + cost_ref[r0 + i, k - 2], diag + cost2[r0 + i, k - 2]
                    )
                    best = jnp.minimum(best, knight + cost5[r0 + i, k - 2])
                    outs[i].append(jnp.minimum(mid[k], best))
            for i in range(2):
                store_row(dst, r0 + i, outs[i])

    @pl.loop(0, SWEEPS // 2)
    def _(step):
        sweep(one, two, 4 * step + 2)
        sweep(two, one, 4 * step + 4)

    @pl.loop(0, rows)
    def _(r):
        for k in range(phases):
            out_ref[r, k] = one[HALO + r, 2 + k]


def finish(cells_ref, times_ref, arrival_ref, gauge_ref, turned, flat):
    rows, phases = times_ref.shape[0], times_ref.shape[1]
    width = arrival_ref.shape[1]
    tiles = width // LANES

    @pl.loop(0, rows)
    def _(r):
        for k in range(phases):
            x = jnp.minimum(times_ref[r, k], clip_value) / clip_value
            shift = tiles
            while shift < LANES:
                x = jnp.minimum(x, pltpu.roll(x, shift, 1))
                shift *= 2
            turned[pl.ds(k, SUBS, stride=phases), :] = x
        flat[pl.ds(pl.multiple_of(r * tiles, tiles), tiles), :] = turned[...].T[:tiles]

    for m in range(tiles):
        arrival_ref[:, m * LANES : (m + 1) * LANES] = flat[pl.ds(m, rows, stride=tiles), :]

    @pl.loop(0, gauge_ref.shape[0])
    def _(g):
        cell = cells_ref[g]
        r = cell // width
        within = (cell % width) % LANES
        gauge_ref[pl.ds(g, 1), :] = times_ref[r, within % phases, pl.ds(within // phases, 1), :]


def on_device(slowness, ocean, start_times, source_cells, gauge_cells, gauge_owner):
    index = lax.axis_index("space")
    count = lax.axis_size("space")
    rows, width = slowness.shape
    sources = start_times.shape[0]
    gauges = gauge_cells.shape[0]
    phases = LANES // SUBS
    tiles = width // LANES
    f32 = jnp.float32
    up = [(i, i + 1) for i in range(count - 1)]
    down = [(j, i) for i, j in up]
    far = jnp.float32(far_value)
    top, bottom = index == 0, index == count - 1

    cost = jnp.where(ocean == 1, slowness, jnp.float32(land_cost))
    cost_prev = jnp.where(top, far, lax.ppermute(cost[rows - HALO :], "space", up))
    cost_next = jnp.where(bottom, far, lax.ppermute(cost[:HALO], "space", down))
    cost = jnp.concatenate([cost_prev, cost, cost_next], axis=0)
    high = rows + 2 * HALO
    fence = jnp.stack([jnp.where(top, far, 0.0), jnp.where(bottom, far, 0.0)]).astype(f32)
    first = (index * (rows * width)).astype(jnp.int32).reshape(1)

    times, packed = pl.pallas_call(
        prepare,
        out_shape=(
            jax.ShapeDtypeStruct((rows, phases, SUBS, LANES), f32),
            jax.ShapeDtypeStruct((high, phases, SUBS, LANES), f32),
        ),
        in_specs=[SMEM, SMEM, VMEM, VMEM],
        out_specs=(VMEM, VMEM),
        scratch_shapes=[
            pltpu.VMEM((high * LANES, LANES), f32),
            pltpu.VMEM((LANES, LANES), f32),
        ],
        compiler_params=PARAMS,
        name="prepare",
    )(first, source_cells, start_times, cost)

    for _ in range(BLOCKS):
        prev = lax.ppermute(times[rows - HALO :], "space", up)
        following = lax.ppermute(times[:HALO], "space", down)
        times = pl.pallas_call(
            functools.partial(relax_block, tiles),
            out_shape=jax.ShapeDtypeStruct(times.shape, f32),
            in_specs=[SMEM, VMEM, VMEM, VMEM, VMEM],
            out_specs=VMEM,
            scratch_shapes=[
                pltpu.VMEM((high, phases + 4, SUBS, LANES), f32),
                pltpu.VMEM((high, phases + 4, SUBS, LANES), f32),
                pltpu.VMEM((high, phases, SUBS, LANES), f32),
                pltpu.VMEM((high, phases, SUBS, LANES), f32),
            ],
            compiler_params=PARAMS,
            name="relax",
        )(fence, prev, times, following, packed)

    arrival, lines = pl.pallas_call(
        finish,
        out_shape=(
            jax.ShapeDtypeStruct((rows, width), f32),
            jax.ShapeDtypeStruct((gauges, LANES), f32),
        ),
        in_specs=[SMEM, VMEM],
        out_specs=(VMEM, VMEM),
        scratch_shapes=[
            pltpu.VMEM((LANES, LANES), f32),
            pltpu.VMEM((rows * tiles, LANES), f32),
        ],
        compiler_params=PARAMS,
        name="finish",
    )(gauge_cells, times)

    tile = (gauge_cells % width) // LANES
    lane = jnp.arange(LANES, dtype=jnp.int32)
    lines = jnp.where(lane[None, :] % tiles == tile[:, None], lines, 0.0)
    values = jnp.sum(lines.reshape(gauges, sources, tiles), axis=2)
    values = jnp.minimum(values, jnp.float32(clip_value)) / clip_value
    owners = gauge_owner[:, 0]
    capacity = max(2, 2 * gauges // count)
    slots = jnp.arange(count * capacity, dtype=jnp.int32)
    same = (owners[:, None] == owners[None, :]) & (
        jnp.arange(gauges)[None, :] < jnp.arange(gauges)[:, None]
    )
    ranks = jnp.sum(same.astype(jnp.int32), axis=1)
    target = owners * capacity + ranks
    placing = (target[:, None] == slots[None, :]).astype(f32)
    placed = lax.dot_general(
        values, placing, (((0,), (0,)), ((), ())),
        precision=lax.Precision.HIGHEST, preferred_element_type=f32,
    )
    received = lax.all_to_all(
        placed.reshape(sources, count, capacity), "space", split_axis=1, concat_axis=1, tiled=True
    )
    return (arrival, received.reshape(1, sources, count * capacity))


def solution(mesh):
    return jax.shard_map(
        on_device,
        mesh=mesh,
        in_specs=(
            P(("groups", "space"), None),
            P(("groups", "space"), None),
            P("groups", "space", None),
            P("groups"),
            P(("groups", "space")),
            P(("groups", "space"), None),
        ),
        out_specs=(P(("groups", "space"), None), P(("groups", "space"), None, None)),
        check_vma=False,
    )
```

```python
import functools

import jax
import jax.numpy as jnp
from jax import lax
from jax.experimental import pallas as pl
from jax.experimental.pallas import tpu as pltpu
from jax.sharding import PartitionSpec as P

SWEEPS = 8
BLOCKS = 3
HALO = 2 * SWEEPS

far_value = 1000000.0
land_cost = 10000.0
clip_value = 48.0
root_two = 1.41421356
root_five = 2.23606798

LANES = 128
SUBS = 8
VMEM = pl.BlockSpec(memory_space=pltpu.VMEM)
SMEM = pl.BlockSpec(memory_space=pltpu.SMEM)
PARAMS = pltpu.CompilerParams(vmem_limit_bytes=48 * 1024 * 1024)


GROUP = 4


def pack_rows(rows, phases, flat, turned, out_ref):
    @pl.loop(0, rows // GROUP)
    def _(group):
        for i in range(GROUP):
            r = group * GROUP + i
            turned[i] = flat[pl.ds(pl.multiple_of(r * LANES, LANES), LANES), :].T
        for i in range(GROUP):
            for k in range(phases):
                out_ref[group * GROUP + i, k] = turned[i, pl.ds(k, SUBS, stride=phases), :]


def prepare_times(first_ref, cells_ref, start_ref, times_ref, flat, turned):
    sources, rows, width = start_ref.shape
    tiles = width // LANES
    rowcol = lax.broadcasted_iota(jnp.int32, (rows, LANES), 0) * width + lax.broadcasted_iota(
        jnp.int32, (rows, LANES), 1
    )
    for s in range(sources):
        offset = cells_ref[s] - first_ref[0]
        for m in range(tiles):
            piece = start_ref[s, :, m * LANES : (m + 1) * LANES]
            piece = jnp.where(rowcol == offset - m * LANES, 0.0, piece)
            flat[pl.ds(s * tiles + m, rows, stride=LANES), :] = piece
    pack_rows(rows, LANES // SUBS, flat, turned, times_ref)


def prepare_cost(sources, prev_ref, cost_ref, next_ref, packed_ref, flat, turned):
    rows, width = cost_ref.shape
    tiles = width // LANES
    for part, ref in enumerate((prev_ref, cost_ref, next_ref)):
        start = (0, HALO, HALO + rows)[part] * LANES
        for m in range(tiles):
            piece = ref[:, m * LANES : (m + 1) * LANES]
            for s in range(sources):
                flat[pl.ds(start + s * tiles + m, ref.shape[0], stride=LANES), :] = piece
    pack_rows(packed_ref.shape[0], LANES // SUBS, flat, turned, packed_ref)


def edge_fixers(tiles):
    sub = lax.broadcasted_iota(jnp.int32, (SUBS, LANES), 0)
    lane = lax.broadcasted_iota(jnp.int32, (SUBS, LANES), 1)
    first = lane % tiles == 0
    last = lane % tiles == tiles - 1
    far = jnp.float32(far_value)

    def from_left(x):
        y = pltpu.roll(x, 1, 0)
        z = jnp.where(first, far, pltpu.roll(y, 1, 1))
        return jnp.where(sub == 0, z, y)

    def from_right(x):
        y = pltpu.roll(x, SUBS - 1, 0)
        z = jnp.where(last, far, pltpu.roll(y, LANES - 1, 1))
        return jnp.where(sub == SUBS - 1, z, y)

    return from_left, from_right


def relax_block(tiles, fence_ref, prev_ref, cur_ref, next_ref, cost_ref, out_ref, one, two, cost2, cost5):
    rows, phases = cur_ref.shape[0], cur_ref.shape[1]
    high = cost_ref.shape[0]
    from_left, from_right = edge_fixers(tiles)

    def store_row(buf, r, vals):
        for k in range(phases):
            buf[r, 2 + k] = vals[k]
        buf[r, 0] = from_left(vals[phases - 2])
        buf[r, 1] = from_left(vals[phases - 1])
        buf[r, phases + 2] = from_right(vals[0])
        buf[r, phases + 3] = from_right(vals[1])

    @pl.loop(0, rows)
    def _(r):
        store_row(one, HALO + r, [cur_ref[r, k] for k in range(phases)])

    @pl.loop(0, HALO)
    def _(r):
        store_row(one, r, [jnp.maximum(prev_ref[r, k], fence_ref[0]) for k in range(phases)])
        store_row(
            one, HALO + rows + r, [jnp.maximum(next_ref[r, k], fence_ref[1]) for k in range(phases)]
        )

    @pl.loop(0, high)
    def _(r):
        for k in range(phases):
            c = cost_ref[r, k]
            cost2[r, k] = c * root_two
            cost5[r, k] = c * root_five

    total = phases + 4

    def sweep(src, dst, lowest):
        groups = (high - 2 * lowest) // GROUP

        def edges(start):
            for i in range(GROUP):
                r = start + i
                dst[r, 0] = from_left(dst[r, phases])
                dst[r, 1] = from_left(dst[r, phases + 1])
                dst[r, phases + 2] = from_right(dst[r, 2])
                dst[r, phases + 3] = from_right(dst[r, 3])

        @pl.loop(0, groups)
        def _(group):
            r0 = lowest + GROUP * group
            edges(jnp.maximum(r0 - GROUP, lowest))
            mid = [[None] * total for _ in range(GROUP)]
            v1 = [[None] * total for _ in range(GROUP)]
            v2 = [[None] * total for _ in range(GROUP)]
            for x in range(total):
                inner = 0 < x < total - 1
                span = range(-2, GROUP + 2) if inner else range(-1, GROUP + 1)
                t = {d: src[r0 + d, x] for d in span}
                for i in range(GROUP):
                    mid[i][x] = t[i]
                    v1[i][x] = jnp.minimum(t[i - 1], t[i + 1])
                    if inner:
                        v2[i][x] = jnp.minimum(t[i - 2], t[i + 2])
                k = x - 2
                if k < 2:
                    continue
                for i in range(GROUP):
                    m, a, b, r = mid[i], v1[i], v2[i], r0 + i
                    near = jnp.minimum(a[k], jnp.minimum(m[k - 1], m[k + 1]))
                    diag = jnp.minimum(a[k - 1], a[k + 1])
                    knight = jnp.minimum(
                        jnp.minimum(a[k - 2], a[k + 2]), jnp.minimum(b[k - 1], b[k + 1])
                    )
                    best = jnp.minimum(near + cost_ref[r, k - 2], diag + cost2[r, k - 2])
                    best = jnp.minimum(best, knight + cost5[r, k - 2])
                    dst[r, k] = jnp.minimum(m[k], best)

        edges(lowest + GROUP * (groups - 1))

    @pl.loop(0, SWEEPS // 2)
    def _(step):
        sweep(one, two, 4 * step + 2)
        sweep(two, one, 4 * step + 4)

    @pl.loop(0, rows)
    def _(r):
        for k in range(phases):
            out_ref[r, k] = one[HALO + r, 2 + k]


def finish(spots_ref, times_ref, arrival_ref, gauge_ref, turned, flat):
    rows, width = arrival_ref.shape
    tiles = width // LANES
    phases = LANES // SUBS

    @pl.loop(0, rows // GROUP)
    def _(group):
        for i in range(GROUP):
            for k in range(phases):
                row = ((group * GROUP + i) * phases + k) * SUBS
                x = times_ref[pl.ds(pl.multiple_of(row, SUBS), SUBS), :]
                shift = tiles
                while shift < LANES:
                    x = jnp.minimum(x, pltpu.roll(x, shift, 1))
                    shift *= 2
                turned[i, pl.ds(k, SUBS, stride=phases), :] = x
        for i in range(GROUP):
            r = group * GROUP + i
            flat[pl.ds(pl.multiple_of(r * tiles, tiles), tiles), :] = turned[i].T[:tiles]

    for m in range(tiles):
        x = flat[pl.ds(m, rows, stride=tiles), :]
        arrival_ref[:, m * LANES : (m + 1) * LANES] = jnp.minimum(x, clip_value) / clip_value

    @pl.loop(0, gauge_ref.shape[0] // SUBS)
    def _(group):
        for i in range(SUBS):
            g = group * SUBS + i
            gauge_ref[pl.ds(g, 1), :] = times_ref[pl.ds(spots_ref[g], 1), :]


def deliver(count, send_ref, recv_ref, send_sems, recv_sems):
    me = lax.axis_index("space")
    barrier = pltpu.get_barrier_semaphore()

    @pl.loop(1, count)
    def _(step):
        peer = lax.rem(me + step, count)
        pl.semaphore_signal(
            barrier, inc=1, device_id={"space": peer}, device_id_type=pl.DeviceIdType.MESH
        )

    pl.semaphore_wait(barrier, count - 1)

    def copy_to(peer):
        return pltpu.make_async_remote_copy(
            src_ref=send_ref.at[peer],
            dst_ref=recv_ref.at[me],
            send_sem=send_sems.at[peer],
            recv_sem=recv_sems.at[me],
            device_id={"space": peer},
            device_id_type=pl.DeviceIdType.MESH,
        )

    @pl.loop(1, count)
    def _(step):
        copy_to(lax.rem(me + step, count)).start()

    recv_ref[me] = send_ref[me]

    @pl.loop(1, count)
    def _(step):
        peer = lax.rem(me + step, count)
        copy_to(peer).wait_send()
        pltpu.make_async_remote_copy(
            src_ref=send_ref.at[peer],
            dst_ref=recv_ref.at[peer],
            send_sem=send_sems.at[peer],
            recv_sem=recv_sems.at[peer],
            device_id={"space": peer},
            device_id_type=pl.DeviceIdType.MESH,
        ).wait_recv()


def on_device(slowness, ocean, start_times, source_cells, gauge_cells, gauge_owner):
    index = lax.axis_index("space")
    count = lax.axis_size("space")
    rows, width = slowness.shape
    sources = start_times.shape[0]
    gauges = gauge_cells.shape[0]
    phases = LANES // SUBS
    tiles = width // LANES
    f32 = jnp.float32
    up = [(i, i + 1) for i in range(count - 1)]
    down = [(j, i) for i, j in up]
    far = jnp.float32(far_value)
    top, bottom = index == 0, index == count - 1

    cost = jnp.where(ocean == 1, slowness, jnp.float32(land_cost))
    cost_prev = jnp.where(top, far, lax.ppermute(cost[rows - HALO :], "space", up))
    cost_next = jnp.where(bottom, far, lax.ppermute(cost[:HALO], "space", down))
    high = rows + 2 * HALO
    fence = jnp.stack([jnp.where(top, far, 0.0), jnp.where(bottom, far, 0.0)]).astype(f32)
    first = (index * (rows * width)).astype(jnp.int32).reshape(1)

    times = pl.pallas_call(
        prepare_times,
        out_shape=jax.ShapeDtypeStruct((rows, phases, SUBS, LANES), f32),
        in_specs=[SMEM, SMEM, VMEM],
        out_specs=VMEM,
        scratch_shapes=[
            pltpu.VMEM((rows * LANES, LANES), f32),
            pltpu.VMEM((GROUP, LANES, LANES), f32),
        ],
        compiler_params=PARAMS,
        name="prepare_times",
    )(first, source_cells, start_times)
    packed = pl.pallas_call(
        functools.partial(prepare_cost, sources),
        out_shape=jax.ShapeDtypeStruct((high, phases, SUBS, LANES), f32),
        in_specs=[VMEM, VMEM, VMEM],
        out_specs=VMEM,
        scratch_shapes=[
            pltpu.VMEM((high * LANES, LANES), f32),
            pltpu.VMEM((GROUP, LANES, LANES), f32),
        ],
        compiler_params=PARAMS,
        cost_estimate=pl.CostEstimate(flops=0, bytes_accessed=20 * 2**20, transcendentals=0),
        name="prepare_cost",
    )(cost_prev, cost, cost_next)

    for _ in range(BLOCKS):
        prev = lax.ppermute(times[rows - HALO :], "space", up)
        following = lax.ppermute(times[:HALO], "space", down)
        times = pl.pallas_call(
            functools.partial(relax_block, tiles),
            out_shape=jax.ShapeDtypeStruct(times.shape, f32),
            in_specs=[SMEM, VMEM, VMEM, VMEM, VMEM],
            out_specs=VMEM,
            scratch_shapes=[
                pltpu.VMEM((high, phases + 4, SUBS, LANES), f32),
                pltpu.VMEM((high, phases + 4, SUBS, LANES), f32),
                pltpu.VMEM((high, phases, SUBS, LANES), f32),
                pltpu.VMEM((high, phases, SUBS, LANES), f32),
            ],
            compiler_params=PARAMS,
            name="relax",
        )(fence, prev, times, following, packed)

    within = gauge_cells % LANES
    spots = ((gauge_cells // width) * phases + within % phases) * SUBS + within // phases
    arrival, lines = pl.pallas_call(
        finish,
        out_shape=(
            jax.ShapeDtypeStruct((rows, width), f32),
            jax.ShapeDtypeStruct((gauges, LANES), f32),
        ),
        in_specs=[SMEM, VMEM],
        out_specs=(VMEM, VMEM),
        scratch_shapes=[
            pltpu.VMEM((GROUP, LANES, LANES), f32),
            pltpu.VMEM((rows * tiles, LANES), f32),
        ],
        compiler_params=PARAMS,
        name="finish",
    )(spots, times.reshape(rows * phases * SUBS, LANES))

    tile = (gauge_cells % width) // LANES
    lane = jnp.arange(LANES, dtype=jnp.int32)
    lines = jnp.where(lane[None, :] % tiles == tile[:, None], lines, 0.0)
    values = jnp.sum(lines.reshape(gauges, sources, tiles), axis=2)
    values = jnp.minimum(values, jnp.float32(clip_value)) / clip_value
    owners = gauge_owner[:, 0]
    capacity = max(2, 2 * gauges // count)
    slots = jnp.arange(count * capacity, dtype=jnp.int32)
    same = (owners[:, None] == owners[None, :]) & (
        jnp.arange(gauges)[None, :] < jnp.arange(gauges)[:, None]
    )
    ranks = jnp.sum(same.astype(jnp.int32), axis=1)
    target = owners * capacity + ranks
    placing = (target[:, None] == slots[None, :]).astype(f32)
    placed = lax.dot_general(
        placing, values, (((0,), (0,)), ((), ())),
        precision=lax.Precision.HIGHEST, preferred_element_type=f32,
    )
    lanes = -(-capacity * sources // LANES) * LANES
    placed = placed.reshape(count, 1, capacity * sources)
    placed = jnp.pad(placed, ((0, 0), (0, 0), (0, lanes - capacity * sources)))
    received = pl.pallas_call(
        functools.partial(deliver, count),
        out_shape=jax.ShapeDtypeStruct(placed.shape, f32),
        in_specs=[VMEM],
        out_specs=VMEM,
        scratch_shapes=[pltpu.SemaphoreType.DMA((count,)), pltpu.SemaphoreType.DMA((count,))],
        compiler_params=pltpu.CompilerParams(collective_id=0, has_side_effects=True),
        name="deliver",
    )(placed)
    received = received[:, 0, : capacity * sources].reshape(count * capacity, sources).T
    return (arrival, received[None])


def solution(mesh):
    return jax.shard_map(
        on_device,
        mesh=mesh,
        in_specs=(
            P(("groups", "space"), None),
            P(("groups", "space"), None),
            P("groups", "space", None),
            P("groups"),
            P(("groups", "space")),
            P(("groups", "space"), None),
        ),
        out_specs=(P(("groups", "space"), None), P(("groups", "space"), None, None)),
        check_vma=False,
    )
```

```python
import functools

import jax
import jax.numpy as jnp
from jax import lax
from jax.experimental import pallas as pl
from jax.experimental.pallas import tpu as pltpu
from jax.sharding import PartitionSpec as P

SWEEPS = 8
BLOCKS = 3
HALO = 2 * SWEEPS
SLAB = 4

far_value = 1000000.0
land_cost = 10000.0
clip_value = 48.0
root_two = 1.41421356
root_five = 2.23606798

LANES = 128
SUBS = 8
GROUP = 8
VMEM = pl.BlockSpec(memory_space=pltpu.VMEM)
SMEM = pl.BlockSpec(memory_space=pltpu.SMEM)
ANY = pl.BlockSpec(memory_space=pl.ANY)
PARAMS = pltpu.CompilerParams(vmem_limit_bytes=48 * 1024 * 1024)
MESH = pl.DeviceIdType.MESH


def window_start(quarter, size):
    return quarter * size - LANES * ((quarter + 2) // 3 + quarter // 3)


def remote(src, dst, send_sem, recv_sem, device):
    return pltpu.make_async_remote_copy(
        src_ref=src,
        dst_ref=dst,
        send_sem=send_sem,
        recv_sem=recv_sem,
        device_id={"space": device},
        device_id_type=MESH,
    )


def signal(barrier, device):
    pl.semaphore_signal(barrier, inc=1, device_id={"space": device}, device_id_type=MESH)


def ends(me, count):
    slab = me // SLAB
    return slab > 0, slab < count // SLAB - 1


def greet(barrier, me, count):
    below, above = ends(me, count)

    @pl.when(below)
    def _():
        signal(barrier, me - SLAB)

    @pl.when(above)
    def _():
        signal(barrier, me + SLAB)

    return below, above


def meet(barrier, me, count, others):
    slabs = count // SLAB
    slab = me // SLAB
    below = (slab + slabs - 1) // slabs
    above = (2 * slabs - 2 - slab) // slabs
    pl.semaphore_wait(barrier, others + below + above)


def trade(me, below, above, downs, ups, send_sems, recv_sems):

    def lower(n):
        return remote(*downs[n], send_sems.at[0, n], recv_sems.at[0, n], me - SLAB)

    def upper(n):
        return remote(*ups[n], send_sems.at[1, n], recv_sems.at[1, n], me + SLAB)

    def landed(side, n, dst, device):
        remote(dst, dst, send_sems.at[side, n], recv_sems.at[side, n], device).wait_recv()

    @pl.when(below)
    def _():
        for n in range(len(downs)):
            lower(n).start()

    @pl.when(above)
    def _():
        for n in range(len(ups)):
            upper(n).start()

    @pl.when(below)
    def _():
        for n in range(len(downs)):
            lower(n).wait_send()
            landed(1, n, ups[n][1], me - SLAB)

    @pl.when(above)
    def _():
        for n in range(len(ups)):
            upper(n).wait_send()
            landed(0, n, downs[n][1], me + SLAB)


def regroup(count, start_ref, cost_ref, info_ref, t_ref, c_ref, g_ref, pt, pc, nt, nc,
            local_sems, send_sems, recv_sems, far_send, far_recv):
    me = lax.axis_index("space")
    base = me // SLAB * SLAB
    p = me % SLAB
    size = start_ref.shape[2] // SLAB
    window = t_ref.shape[3]
    barrier = pltpu.get_barrier_semaphore()
    for o in range(1, SLAB):
        signal(barrier, base + (p + o) % SLAB)
    below, above = greet(barrier, me, count)
    meet(barrier, me, count, SLAB - 1)

    def pieces(q):
        cols = pl.ds(pl.multiple_of(window_start(q, size), LANES), window)
        return (
            (start_ref.at[:, :, cols], t_ref.at[p]),
            (cost_ref.at[:, cols], c_ref.at[p]),
            (info_ref, g_ref.at[p]),
        )

    def outgoing(o):
        q = (p + o) % SLAB
        return [
            remote(src, dst, send_sems.at[o - 1, n], recv_sems.at[p, n], base + q)
            for n, (src, dst) in enumerate(pieces(q))
        ]

    local = [
        pltpu.make_async_copy(src, dst, local_sems.at[n]) for n, (src, dst) in enumerate(pieces(p))
    ]
    for o in (2, 1, 3):
        for c in outgoing(o):
            c.start()
    for c in local:
        c.start()
    for c in local:
        c.wait()
    for o in range(1, SLAB):
        q = (p + o) % SLAB
        for n, ref in enumerate((t_ref, c_ref, g_ref)):
            remote(ref.at[q], ref.at[q], send_sems.at[o - 1, n], recv_sems.at[q, n], base + q).wait_recv()
    trade(me, below, above,
          ((t_ref.at[0], nt), (c_ref.at[0], nc)),
          ((t_ref.at[SLAB - 1], pt), (c_ref.at[SLAB - 1], pc)), far_send, far_recv)
    for o in range(1, SLAB):
        for c in outgoing(o):
            c.wait_send()


def swap(count, times_ref, prev_ref, next_ref, far_send, far_recv):
    me = lax.axis_index("space")
    barrier = pltpu.get_barrier_semaphore()
    below, above = greet(barrier, me, count)
    meet(barrier, me, count, 0)
    rows = times_ref.shape[0]
    trade(me, below, above,
          ((times_ref.at[pl.ds(0, HALO)], next_ref),),
          ((times_ref.at[pl.ds(rows - HALO, HALO)], prev_ref),), far_send, far_recv)


def selection(phases, back):
    size = phases * LANES
    packed = lax.broadcasted_iota(jnp.int32, (size, size), 0 if back else 1)
    plain = lax.broadcasted_iota(jnp.int32, (size, size), 1 if back else 0)
    return jnp.where(plain == packed % LANES * phases + packed // LANES, 1.0, 0.0)


def prepare(width, first_ref, cells_ref, fence_ref, t_ref, c_ref, pt, pc, nt, nc, times_ref,
            packed_ref, choose):
    _, sources, rows, window = t_ref.shape
    half = window // 2
    phases = half // LANES
    choose[...] = selection(phases, False)
    row = lax.broadcasted_iota(jnp.int32, (rows, half), 0)
    col = lax.broadcasted_iota(jnp.int32, (rows, half), 1)
    place = row * width + col
    far = jnp.float32(far_value)

    def arrange(x):
        return jnp.dot(
            x, choose[...], precision=lax.Precision.HIGHEST, preferred_element_type=jnp.float32
        )

    def put(ref, block, h, s, y, k):
        start = (block * rows * phases + k) * SUBS + s * 2 + h
        ref[pl.ds(start, rows, stride=phases * SUBS), :] = y

    for block in range(SLAB + 2):
        outside = None
        if block in (0, SLAB + 1):
            outside = fence_ref[0 if block == 0 else 1] > 0.0
        for h in range(2):
            cols = slice(h * half, (h + 1) * half)
            xs = []
            for s in range(sources):
                if block == 0:
                    x = pt[s, :, cols]
                elif block == SLAB + 1:
                    x = nt[s, :, cols]
                else:
                    x = t_ref[block - 1, s, :, cols]
                offset = cells_ref[s] - (first_ref[0] + (block - 1) * rows * width + h * half)
                x = jnp.where(place == offset, 0.0, x)
                xs.append(x)
            if block == 0:
                c = pc[:, cols]
            elif block == SLAB + 1:
                c = nc[:, cols]
            else:
                c = c_ref[block - 1, :, cols]
            xs.append(c)
            if outside is not None:
                xs = [jnp.where(outside, far, x) for x in xs]
            y = arrange(jnp.concatenate(xs, axis=0))
            for k in range(phases):
                for s in range(sources):
                    put(times_ref, block, h, s, y[s * rows : (s + 1) * rows, k * LANES : (k + 1) * LANES], k)
                    put(packed_ref, block, h, s, y[sources * rows :, k * LANES : (k + 1) * LANES], k)


def edge_fixers():
    sub = lax.broadcasted_iota(jnp.int32, (SUBS, LANES), 0)
    lane = lax.broadcasted_iota(jnp.int32, (SUBS, LANES), 1)
    far = jnp.float32(far_value)

    def from_left(x):
        y = pltpu.roll(x, 1, 1)
        z = jnp.where(sub % 2 == 0, far, pltpu.roll(y, 1, 0))
        return jnp.where(lane == 0, z, y)

    def from_right(x):
        y = pltpu.roll(x, LANES - 1, 1)
        z = jnp.where(sub % 2 == 1, far, pltpu.roll(y, SUBS - 1, 0))
        return jnp.where(lane == LANES - 1, z, y)

    return from_left, from_right


def relax_block(fence_ref, prev_ref, cur_ref, next_ref, cost_ref, out_ref, one, two, cost2, cost5):
    rows, phases = cur_ref.shape[0], cur_ref.shape[1]
    high = cost_ref.shape[0]
    total = phases + 4
    far = jnp.float32(far_value)
    from_left, from_right = edge_fixers()

    def store_row(buf, r, vals):
        for k in range(phases):
            buf[r, 2 + k] = vals[k]
        buf[r, 0] = from_left(vals[phases - 2])
        buf[r, 1] = from_left(vals[phases - 1])
        buf[r, phases + 2] = from_right(vals[0])
        buf[r, phases + 3] = from_right(vals[1])

    @pl.loop(0, rows // 4)
    def _(g):
        for i in range(4):
            r = 4 * g + i
            store_row(one, HALO + r, [cur_ref[r, k] for k in range(phases)])

    for ref, start, n in ((prev_ref, 0, 0), (next_ref, HALO + rows, 1)):

        @pl.loop(0, HALO // 4)
        def _(g):
            for i in range(4):
                r = 4 * g + i
                vals = [jnp.where(fence_ref[n] > 0.0, far, ref[r, k]) for k in range(phases)]
                store_row(one, start + r, vals)

    @pl.loop(0, high // 4)
    def _(g):
        for i in range(4):
            for k in range(phases):
                c = cost_ref[4 * g + i, k]
                cost2[4 * g + i, k] = c * root_two
                cost5[4 * g + i, k] = c * root_five

    def sweep(src, dst, lowest):
        groups = (high - 2 * lowest + GROUP - 1) // GROUP

        def begin(group):
            return jnp.minimum(lowest + GROUP * group, high - lowest - GROUP)

        def edges(start):
            for i in range(GROUP):
                r = start + i
                dst[r, 0] = from_left(dst[r, phases])
                dst[r, 1] = from_left(dst[r, phases + 1])
                dst[r, phases + 2] = from_right(dst[r, 2])
                dst[r, phases + 3] = from_right(dst[r, 3])

        @pl.loop(0, groups)
        def _(group):
            r0 = begin(group)
            edges(begin(jnp.maximum(group - 1, 0)))
            t = {}

            def load(d):
                inner = range(1, total - 1) if d in (-2, GROUP + 1) else range(total)
                t[d] = {x: src[r0 + d, x] for x in inner}

            for d in (-2, -1, 0, 1):
                load(d)
            for i in range(GROUP):
                load(i + 2)
                r = r0 + i
                m = t[i]
                a = [jnp.minimum(t[i - 1][x], t[i + 1][x]) for x in range(total)]
                b = {x: jnp.minimum(t[i - 2][x], t[i + 2][x]) for x in range(1, total - 1)}
                for k in range(2, phases + 2):
                    near = jnp.minimum(a[k], jnp.minimum(m[k - 1], m[k + 1]))
                    diag = jnp.minimum(a[k - 1], a[k + 1])
                    knight = jnp.minimum(
                        jnp.minimum(a[k - 2], a[k + 2]), jnp.minimum(b[k - 1], b[k + 1])
                    )
                    best = jnp.minimum(near + cost_ref[r, k - 2], diag + cost2[r, k - 2])
                    best = jnp.minimum(best, knight + cost5[r, k - 2])
                    dst[r, k] = jnp.minimum(m[k], best)

        edges(begin(groups - 1))

    @pl.loop(0, SWEEPS // 2)
    def _(step):
        sweep(one, two, 4 * step + 2)
        sweep(two, one, 4 * step + 4)

    @pl.loop(0, rows)
    def _(r):
        for k in range(phases):
            out_ref[r, k] = one[HALO + r, 2 + k]


def finish(spots_ref, turns_ref, times_ref, arrival_ref, gauge_ref, least, choose):
    slab, rows, window = arrival_ref.shape
    half = window // 2
    phases = half // LANES
    choose[...] = selection(phases, True)
    steps = slab * rows * phases
    lane = lax.broadcasted_iota(jnp.int32, (SUBS, LANES), 1)

    @pl.loop(0, steps // SUBS)
    def _(group):
        for i in range(SUBS):
            row = pl.ds(pl.multiple_of((group * SUBS + i) * SUBS, SUBS), SUBS)
            x = times_ref[row, :]
            x = jnp.minimum(x, pltpu.roll(x, 2, 0))
            least[row, :] = jnp.minimum(x, pltpu.roll(x, 4, 0))

    for h in range(2):
        x = jnp.concatenate(
            [least[pl.ds(k * SUBS + h, slab * rows, stride=phases * SUBS), :] for k in range(phases)],
            axis=1,
        )
        x = jnp.minimum(x, clip_value) / clip_value
        y = jnp.dot(x, choose[...], precision=lax.Precision.HIGHEST, preferred_element_type=jnp.float32)
        for b in range(slab):
            arrival_ref[b, :, h * half : (h + 1) * half] = y[b * rows : (b + 1) * rows]

    gauges = gauge_ref.shape[2]
    for b in range(slab):
        for start in range(0, gauges, LANES):

            def step(group, acc):
                for i in range(SUBS):
                    n = group * SUBS + i
                    g = b * gauges + start + n
                    x = times_ref[pl.ds(pl.multiple_of(spots_ref[g], SUBS), SUBS), :]
                    x = pltpu.roll(x, turns_ref[g], 1)
                    acc = jnp.where(lane == n, x, acc)
                return acc

            acc = lax.fori_loop(0, LANES // SUBS, step, jnp.zeros((SUBS, LANES), jnp.float32))
            gauge_ref[b, :, start : start + LANES] = acc


def deliver(count, size, arrival_ref, send_ref, out_ref, recv_ref, send_sems, recv_sems,
            slab_send, slab_recv, local_sems):
    me = lax.axis_index("space")
    base = me // SLAB * SLAB
    p = me % SLAB
    barrier = pltpu.get_barrier_semaphore()

    @pl.loop(1, count)
    def _(step):
        signal(barrier, lax.rem(me + step, count))

    pl.semaphore_wait(barrier, count - 1)
    mine = pl.ds(pl.multiple_of(p * size - window_start(p, size), LANES), size)

    def columns(q):
        return pl.ds(pl.multiple_of(q * size, LANES), size)

    def block(o):
        q = (p + o) % SLAB
        return remote(
            arrival_ref.at[q, :, mine], out_ref.at[:, columns(p)],
            slab_send.at[o - 1], slab_recv.at[p], base + q,
        )

    def copy_to(peer):
        return remote(send_ref.at[peer], recv_ref.at[me], send_sems.at[peer], recv_sems.at[me], peer)

    for o in (2, 1, 3):
        block(o).start()

    @pl.loop(1, count)
    def _(step):
        copy_to(lax.rem(me + step, count)).start()

    own = pltpu.make_async_copy(arrival_ref.at[p, :, mine], out_ref.at[:, columns(p)], local_sems.at[0])
    kept = pltpu.make_async_copy(send_ref.at[me], recv_ref.at[me], local_sems.at[1])
    own.start()
    kept.start()
    own.wait()
    kept.wait()

    @pl.loop(1, count)
    def _(step):
        peer = lax.rem(me + step, count)
        copy_to(peer).wait_send()
        remote(send_ref.at[peer], recv_ref.at[peer], send_sems.at[peer], recv_sems.at[peer], peer).wait_recv()

    for o in range(1, SLAB):
        q = (p + o) % SLAB
        block(o).wait_send()
        remote(
            arrival_ref.at[q, :, mine], out_ref.at[:, columns(q)],
            slab_send.at[o - 1], slab_recv.at[q], base + q,
        ).wait_recv()


def on_device(slowness, ocean, start_times, source_cells, gauge_cells, gauge_owner):
    index = lax.axis_index("space")
    count = lax.axis_size("space")
    rows, width = slowness.shape
    sources = start_times.shape[0]
    gauges = gauge_cells.shape[0]
    size = width // SLAB
    window = size + 2 * LANES
    half = window // 2
    phases = half // LANES
    f32 = jnp.float32
    high = rows * SLAB + 2 * HALO
    far = jnp.float32(far_value)
    q = index % SLAB
    slab = index // SLAB
    left = window_start(q, size)

    cost = jnp.where(ocean == 1, slowness, jnp.float32(land_cost))
    info = jnp.stack([gauge_cells, gauge_owner[:, 0]])[:, None, :]
    fence = jnp.stack([jnp.where(slab == 0, 1.0, 0.0), jnp.where(slab == count // SLAB - 1, 1.0, 0.0)])
    fence = fence.astype(f32)
    first = (slab * (SLAB * rows * width) + left).astype(jnp.int32).reshape(1)
    dma = pltpu.SemaphoreType.DMA

    piece_t = jax.ShapeDtypeStruct((sources, rows, window), f32)
    piece_c = jax.ShapeDtypeStruct((rows, window), f32)
    t4, c4, g4, pt, pc, nt, nc = pl.pallas_call(
        functools.partial(regroup, count),
        out_shape=(
            jax.ShapeDtypeStruct((SLAB,) + piece_t.shape, f32),
            jax.ShapeDtypeStruct((SLAB,) + piece_c.shape, f32),
            jax.ShapeDtypeStruct((SLAB,) + info.shape, jnp.int32),
            piece_t, piece_c, piece_t, piece_c,
        ),
        in_specs=[ANY] * 3,
        out_specs=(ANY,) * 7,
        scratch_shapes=[dma((3,)), dma((SLAB - 1, 3)), dma((SLAB, 3)), dma((2, 2)), dma((2, 2))],
        compiler_params=pltpu.CompilerParams(collective_id=0, has_side_effects=True),
        name="regroup",
    )(start_times, cost, info)

    flat = jax.ShapeDtypeStruct((high * phases * SUBS, LANES), f32)
    times, packed = pl.pallas_call(
        functools.partial(prepare, width),
        out_shape=(flat, flat),
        in_specs=[SMEM] * 3 + [VMEM] * 6,
        out_specs=(VMEM, VMEM),
        scratch_shapes=[pltpu.VMEM((half, half), f32)],
        compiler_params=PARAMS,
        name="prepare",
    )(first, source_cells, fence, t4, c4, pt, pc, nt, nc)
    packed = packed.reshape(high, phases, SUBS, LANES)
    times = times.reshape(high, phases, SUBS, LANES)
    prev, times, following = times[:HALO], times[HALO : high - HALO], times[high - HALO :]

    for block in range(BLOCKS):
        if block:
            halo = jax.ShapeDtypeStruct((HALO,) + times.shape[1:], f32)
            prev, following = pl.pallas_call(
                functools.partial(swap, count),
                out_shape=(halo, halo),
                in_specs=[ANY],
                out_specs=(ANY, ANY),
                scratch_shapes=[dma((2, 1)), dma((2, 1))],
                compiler_params=pltpu.CompilerParams(collective_id=block, has_side_effects=True),
                name=f"swap_{block}",
            )(times)
        times = pl.pallas_call(
            relax_block,
            out_shape=jax.ShapeDtypeStruct(times.shape, f32),
            in_specs=[SMEM, VMEM, VMEM, VMEM, VMEM],
            out_specs=VMEM,
            scratch_shapes=[
                pltpu.VMEM((high, phases + 4, SUBS, LANES), f32),
                pltpu.VMEM((high, phases + 4, SUBS, LANES), f32),
                pltpu.VMEM((high, phases, SUBS, LANES), f32),
                pltpu.VMEM((high, phases, SUBS, LANES), f32),
            ],
            compiler_params=PARAMS,
            name="relax",
        )(fence, prev, times, following, packed)

    cells, owners = g4[:, 0, 0], g4[:, 1, 0]
    column = cells % width
    inside = column // size == q
    local = jnp.clip(column - left, 0, window - 1)
    where = local % half
    grid_row = jnp.arange(SLAB, dtype=jnp.int32)[:, None] * rows + cells // width
    spots = (grid_row * phases + where % phases) * SUBS
    turns = (jnp.arange(gauges, dtype=jnp.int32)[None, :] - where // phases) % LANES
    arrival, lines = pl.pallas_call(
        finish,
        out_shape=(
            jax.ShapeDtypeStruct((SLAB, rows, window), f32),
            jax.ShapeDtypeStruct((SLAB, SUBS, gauges), f32),
        ),
        in_specs=[SMEM, SMEM, VMEM],
        out_specs=(VMEM, VMEM),
        scratch_shapes=[
            pltpu.VMEM((SLAB * rows * phases * SUBS, LANES), f32),
            pltpu.VMEM((half, half), f32),
        ],
        compiler_params=PARAMS,
        name="finish",
    )(spots.reshape(-1), turns.reshape(-1), times.reshape(-1, LANES))

    lines = lines.reshape(SLAB, sources, 2, gauges)
    values = jnp.where((local // half == 0)[:, None, :], lines[:, :, 0], lines[:, :, 1])
    values = jnp.minimum(values, jnp.float32(clip_value)) / clip_value
    values = jnp.where(inside[:, None, :], values, 0.0)
    capacity = max(2, 2 * gauges // count)
    slots = jnp.arange(count * capacity, dtype=jnp.int32)
    same = (owners[:, :, None] == owners[:, None, :]) & (
        jnp.arange(gauges)[None, :] < jnp.arange(gauges)[:, None]
    )
    ranks = jnp.sum(same.astype(jnp.int32), axis=2)
    target = owners * capacity + ranks
    placing = (target[:, :, None] == slots[None, None, :]).astype(f32)
    placed = jnp.einsum(
        "bsg,bgt->bst", values, placing,
        precision=lax.Precision.HIGHEST, preferred_element_type=f32,
    )
    amount = SLAB * sources * capacity
    lanes = -(-amount // LANES) * LANES
    placed = placed.reshape(SLAB, sources, count, capacity).transpose(2, 0, 1, 3)
    placed = jnp.pad(placed.reshape(count, 1, amount), ((0, 0), (0, 0), (0, lanes - amount)))
    arrival, received = pl.pallas_call(
        functools.partial(deliver, count, size),
        out_shape=(jax.ShapeDtypeStruct((rows, width), f32), jax.ShapeDtypeStruct(placed.shape, f32)),
        in_specs=[VMEM, VMEM],
        out_specs=(VMEM, VMEM),
        scratch_shapes=[dma((count,)), dma((count,)), dma((SLAB - 1,)), dma((SLAB,)), dma((2,))],
        compiler_params=pltpu.CompilerParams(collective_id=BLOCKS, has_side_effects=True),
        name="deliver",
    )(arrival, placed)
    received = received[:, 0, :amount].reshape(count // SLAB, SLAB, SLAB, sources, capacity)
    received = jnp.sum(received, axis=1).transpose(2, 0, 1, 3)
    return (arrival, received.reshape(1, sources, count * capacity))


def solution(mesh):
    return jax.shard_map(
        on_device,
        mesh=mesh,
        in_specs=(
            P(("groups", "space"), None),
            P(("groups", "space"), None),
            P("groups", "space", None),
            P("groups"),
            P(("groups", "space")),
            P(("groups", "space"), None),
        ),
        out_specs=(P(("groups", "space"), None), P(("groups", "space"), None, None)),
        check_vma=False,
    )
```

```python
import functools

import jax
import jax.numpy as jnp
from jax import lax
from jax.experimental import pallas as pl
from jax.experimental.pallas import tpu as pltpu
from jax.sharding import PartitionSpec as P

SWEEPS = 8
BLOCKS = 3
HALO = 2 * SWEEPS
SLAB = 4

far_value = 1000000.0
land_cost = 10000.0
clip_value = 48.0
root_two = 1.41421356
root_five = 2.23606798

LANES = 128
SUBS = 8
GROUP = 8
EDGE = 4
VMEM = pl.BlockSpec(memory_space=pltpu.VMEM)
SMEM = pl.BlockSpec(memory_space=pltpu.SMEM)
ANY = pl.BlockSpec(memory_space=pl.ANY)
PARAMS = pltpu.CompilerParams(vmem_limit_bytes=48 * 1024 * 1024)
MESH = pl.DeviceIdType.MESH


def window_start(quarter, size):
    return quarter * size - LANES * ((quarter + 2) // 3 + quarter // 3)


def remote(src, dst, send_sem, recv_sem, device):
    return pltpu.make_async_remote_copy(
        src_ref=src,
        dst_ref=dst,
        send_sem=send_sem,
        recv_sem=recv_sem,
        device_id={"space": device},
        device_id_type=MESH,
    )


def signal(barrier, device):
    pl.semaphore_signal(barrier, inc=1, device_id={"space": device}, device_id_type=MESH)


def ends(me, count):
    slab = me // SLAB
    return slab > 0, slab < count // SLAB - 1


def greet(barrier, me, count):
    below, above = ends(me, count)

    @pl.when(below)
    def _():
        signal(barrier, me - SLAB)

    @pl.when(above)
    def _():
        signal(barrier, me + SLAB)

    return below, above


def meet(barrier, me, count, others):
    slabs = count // SLAB
    slab = me // SLAB
    below = (slab + slabs - 1) // slabs
    above = (2 * slabs - 2 - slab) // slabs
    pl.semaphore_wait(barrier, others + below + above)


def selection(phases, back):
    size = phases * LANES
    packed = lax.broadcasted_iota(jnp.int32, (size, size), 0 if back else 1)
    plain = lax.broadcasted_iota(jnp.int32, (size, size), 1 if back else 0)
    return jnp.where(plain == packed % LANES * phases + packed // LANES, 1.0, 0.0)


def gather(count, first_ref, cells_ref, start_ref, cost_ref, info_ref, times_ref, packed_ref, g_ref,
           choose, t_ref, c_ref, pc, nc, local_sems, send_sems, recv_sems, far_send, far_recv):
    me = lax.axis_index("space")
    base = me // SLAB * SLAB
    p = me % SLAB
    _, sources, rows, window = t_ref.shape
    width = start_ref.shape[2]
    size = width // SLAB
    barrier = pltpu.get_barrier_semaphore()
    for o in range(1, SLAB):
        signal(barrier, base + (p + o) % SLAB)
    below, above = greet(barrier, me, count)
    meet(barrier, me, count, SLAB - 1)
    kinds = (c_ref, g_ref, t_ref)

    def piece(q, n):
        cols = pl.ds(pl.multiple_of(window_start(q, size), LANES), window)
        return (cost_ref.at[:, cols], info_ref, start_ref.at[:, :, cols])[n], kinds[n].at[p]

    def outgoing(o, n):
        q = (p + o) % SLAB
        return remote(*piece(q, n), send_sems.at[o - 1, n], recv_sems.at[p, n], base + q)

    def arrived(o, n):
        q = (p + o) % SLAB
        ref = kinds[n].at[q]
        remote(ref, ref, send_sems.at[o - 1, n], recv_sems.at[q, n], base + q).wait_recv()

    local = [pltpu.make_async_copy(*piece(p, n), local_sems.at[n]) for n in range(3)]
    for n in range(3):
        for o in (2, 1, 3):
            outgoing(o, n).start()
        local[n].start()
    half = window // 2
    phases = half // LANES
    choose[...] = selection(phases, False)
    row = lax.broadcasted_iota(jnp.int32, (rows, half), 0)
    col = lax.broadcasted_iota(jnp.int32, (rows, half), 1)
    place = row * width + col
    far = jnp.float32(far_value)
    chunk = rows * phases * SUBS

    def arrange(x):
        return jnp.dot(
            x, choose[...], precision=lax.Precision.HIGHEST, preferred_element_type=jnp.float32
        )

    def put(ref, start, n, y):
        for k in range(phases):
            ref[pl.ds(start + k * SUBS + n, rows, stride=phases * SUBS), :] = y[:, k * LANES : (k + 1) * LANES]

    def pack_times(q):
        for h in range(2):
            cols = slice(h * half, (h + 1) * half)
            xs = []
            for s in range(sources):
                offset = cells_ref[s] - (first_ref[0] + q * (rows * width) + h * half)
                xs.append(jnp.where(place == offset, 0.0, t_ref[q, s, :, cols]))
            y = arrange(jnp.concatenate(xs, axis=0))
            for s in range(sources):
                put(times_ref, q * chunk, s * 2 + h, y[s * rows : (s + 1) * rows])

    def pack_costs(xs, starts):
        for h in range(2):
            y = arrange(jnp.concatenate([x[:, h * half : (h + 1) * half] for x in xs], axis=0))
            for n, start in enumerate(starts):
                for s in range(sources):
                    put(packed_ref, start, s * 2 + h, y[n * rows : (n + 1) * rows])

    local[2].wait()
    pack_times(p)
    local[0].wait()
    local[1].wait()
    for o in range(1, SLAB):
        arrived(o, 0)
        arrived(o, 1)

    def lower():
        return remote(c_ref.at[0], nc, far_send.at[0], far_recv.at[0], me - SLAB)

    def upper():
        return remote(c_ref.at[SLAB - 1], pc, far_send.at[1], far_recv.at[1], me + SLAB)

    @pl.when(below)
    def _():
        lower().start()

    @pl.when(above)
    def _():
        upper().start()

    pack_costs([c_ref[q] for q in range(SLAB)], [(q + 1) * chunk for q in range(SLAB)])

    @pl.when(below)
    def _():
        lower().wait_send()
        remote(pc, pc, far_send.at[1], far_recv.at[1], me - SLAB).wait_recv()

    @pl.when(above)
    def _():
        upper().wait_send()
        remote(nc, nc, far_send.at[0], far_recv.at[0], me + SLAB).wait_recv()

    pack_costs(
        [jnp.where(below, pc[...], far), jnp.where(above, nc[...], far)], [0, (SLAB + 1) * chunk]
    )
    for o in (1, 3, 2):
        arrived(o, 2)
        pack_times((p + o) % SLAB)
    for o in range(1, SLAB):
        for n in range(3):
            outgoing(o, n).wait_send()


def edge_fixers():
    sub = lax.broadcasted_iota(jnp.int32, (SUBS, LANES), 0)
    lane = lax.broadcasted_iota(jnp.int32, (SUBS, LANES), 1)
    far = jnp.float32(far_value)

    def from_left(x):
        y = pltpu.roll(x, 1, 1)
        z = jnp.where(sub % 2 == 0, far, pltpu.roll(y, 1, 0))
        return jnp.where(lane == 0, z, y)

    def from_right(x):
        y = pltpu.roll(x, LANES - 1, 1)
        z = jnp.where(sub % 2 == 1, far, pltpu.roll(y, SUBS - 1, 0))
        return jnp.where(lane == LANES - 1, z, y)

    return from_left, from_right


def march(count, times_ref, cost_ref, out_ref, one, two, staged, landed, send_sems, recv_sems):
    me = lax.axis_index("space")
    barrier = pltpu.get_barrier_semaphore()
    below, above = greet(barrier, me, count)
    rows, phases = times_ref.shape[0], times_ref.shape[1]
    high = cost_ref.shape[0]
    total = phases + 4
    far = jnp.float32(far_value)
    from_left, from_right = edge_fixers()

    @pl.loop(0, rows // 4)
    def _(g):
        for i in range(4):
            r = HALO + 4 * g + i
            vals = [times_ref[4 * g + i, k] for k in range(phases)]
            for k in range(phases):
                one[r, 2 + k] = vals[k]
            one[r, 0] = from_left(vals[phases - 2])
            one[r, 1] = from_left(vals[phases - 1])
            one[r, phases + 2] = from_right(vals[0])
            one[r, phases + 3] = from_right(vals[1])

    meet(barrier, me, count, 0)

    def sweep(src, dst, lo, hi, size):
        groups = (hi - lo + size - 1) // size

        def begin(group):
            return jnp.minimum(lo + size * group, hi - size)

        def edges(start):
            for i in range(size):
                r = start + i
                dst[r, 0] = from_left(dst[r, phases])
                dst[r, 1] = from_left(dst[r, phases + 1])
                dst[r, phases + 2] = from_right(dst[r, 2])
                dst[r, phases + 3] = from_right(dst[r, 3])

        @pl.loop(0, groups)
        def _(group):
            r0 = begin(group)
            edges(begin(jnp.maximum(group - 1, 0)))
            t = {}

            def load(d):
                inner = range(1, total - 1) if d in (-2, size + 1) else range(total)
                t[d] = {x: src[r0 + d, x] for x in inner}

            for d in (-2, -1, 0, 1):
                load(d)
            for i in range(size):
                load(i + 2)
                r = r0 + i
                m = t[i]
                a = [jnp.minimum(t[i - 1][x], t[i + 1][x]) for x in range(total)]
                b = {x: jnp.minimum(t[i - 2][x], t[i + 2][x]) for x in range(1, total - 1)}
                for k in range(2, phases + 2):
                    c = cost_ref[r, k - 2]
                    near = jnp.minimum(a[k], jnp.minimum(m[k - 1], m[k + 1]))
                    diag = jnp.minimum(a[k - 1], a[k + 1])
                    knight = jnp.minimum(
                        jnp.minimum(a[k - 2], a[k + 2]), jnp.minimum(b[k - 1], b[k + 1])
                    )
                    best = jnp.minimum(near + c, diag + c * root_two)
                    best = jnp.minimum(best, knight + c * root_five)
                    dst[r, k] = jnp.minimum(m[k], best)

        edges(begin(groups - 1))

    def inner(src, dst, j):
        sweep(src, dst, HALO + 4 * j, high - HALO - 4 * j, GROUP)

    def outer(src, dst, j):
        sweep(src, dst, 2 * j, HALO + 4 * j, EDGE)
        sweep(src, dst, high - HALO - 4 * j, high - 2 * j, EDGE)

    last = (rows - GROUP) // 8

    @pl.loop(0, BLOCKS)
    def _(block):
        def down():
            return remote(staged.at[0], landed.at[block, 1], send_sems.at[block, 0],
                          recv_sems.at[block, 1], me - SLAB)

        def up():
            return remote(staged.at[1], landed.at[block, 0], send_sems.at[block, 1],
                          recv_sems.at[block, 0], me + SLAB)

        @pl.loop(0, HALO)
        def _(r):
            for x in range(total):
                staged[0, r, x] = one[HALO + r, x]
                staged[1, r, x] = one[high - 2 * HALO + r, x]

        @pl.when(below)
        def _():
            down().start()

        @pl.when(above)
        def _():
            up().start()

        inner_pairs = min(SWEEPS, last) // 2

        @pl.loop(0, inner_pairs)
        def _(step):
            inner(one, two, 2 * step + 1)
            inner(two, one, 2 * step + 2)

        for j in range(2 * inner_pairs + 1, min(SWEEPS, last) + 1):
            inner(one, two, j)

        @pl.when(below)
        def _():
            down().wait_send()
            remote(landed.at[block, 0], landed.at[block, 0], send_sems.at[block, 0],
                   recv_sems.at[block, 0], me - SLAB).wait_recv()

        @pl.when(above)
        def _():
            up().wait_send()
            remote(landed.at[block, 1], landed.at[block, 1], send_sems.at[block, 1],
                   recv_sems.at[block, 1], me + SLAB).wait_recv()

        @pl.loop(0, HALO)
        def _(r):
            for x in range(total):
                one[r, x] = jnp.where(below, landed[block, 0, r, x], far)
                one[high - HALO + r, x] = jnp.where(above, landed[block, 1, r, x], far)

        @pl.loop(0, SWEEPS // 2)
        def _(step):
            outer(one, two, 2 * step + 1)
            outer(two, one, 2 * step + 2)

    @pl.loop(0, rows)
    def _(r):
        for k in range(phases):
            out_ref[r, k] = one[HALO + r, 2 + k]


def finish(spots_ref, turns_ref, times_ref, arrival_ref, gauge_ref, least, choose):
    slab, rows, window = arrival_ref.shape
    half = window // 2
    phases = half // LANES
    choose[...] = selection(phases, True)
    steps = slab * rows * phases
    lane = lax.broadcasted_iota(jnp.int32, (SUBS, LANES), 1)

    @pl.loop(0, steps // SUBS)
    def _(group):
        for i in range(SUBS):
            row = pl.ds(pl.multiple_of((group * SUBS + i) * SUBS, SUBS), SUBS)
            x = times_ref[row, :]
            x = jnp.minimum(x, pltpu.roll(x, 2, 0))
            least[row, :] = jnp.minimum(x, pltpu.roll(x, 4, 0))

    for h in range(2):
        x = jnp.concatenate(
            [least[pl.ds(k * SUBS + h, slab * rows, stride=phases * SUBS), :] for k in range(phases)],
            axis=1,
        )
        x = jnp.minimum(x, clip_value) / clip_value
        y = jnp.dot(x, choose[...], precision=lax.Precision.HIGHEST, preferred_element_type=jnp.float32)
        for b in range(slab):
            arrival_ref[b, :, h * half : (h + 1) * half] = y[b * rows : (b + 1) * rows]

    gauges = gauge_ref.shape[2]
    for b in range(slab):
        for start in range(0, gauges, LANES):

            def step(group, acc):
                for i in range(SUBS):
                    n = group * SUBS + i
                    g = b * gauges + start + n
                    x = times_ref[pl.ds(pl.multiple_of(spots_ref[g], SUBS), SUBS), :]
                    x = pltpu.roll(x, turns_ref[g], 1)
                    acc = jnp.where(lane == n, x, acc)
                return acc

            acc = lax.fori_loop(0, LANES // SUBS, step, jnp.zeros((SUBS, LANES), jnp.float32))
            gauge_ref[b, :, start : start + LANES] = acc


def deliver(count, size, arrival_ref, send_ref, out_ref, recv_ref, send_sems, recv_sems,
            slab_send, slab_recv, local_sems):
    me = lax.axis_index("space")
    base = me // SLAB * SLAB
    p = me % SLAB
    barrier = pltpu.get_barrier_semaphore()

    @pl.loop(1, count)
    def _(step):
        signal(barrier, lax.rem(me + step, count))

    pl.semaphore_wait(barrier, count - 1)
    mine = pl.ds(pl.multiple_of(p * size - window_start(p, size), LANES), size)

    def columns(q):
        return pl.ds(pl.multiple_of(q * size, LANES), size)

    def block(o):
        q = (p + o) % SLAB
        return remote(
            arrival_ref.at[q, :, mine], out_ref.at[:, columns(p)],
            slab_send.at[o - 1], slab_recv.at[p], base + q,
        )

    def copy_to(peer):
        return remote(send_ref.at[peer], recv_ref.at[me], send_sems.at[peer], recv_sems.at[me], peer)

    for o in (2, 1, 3):
        block(o).start()

    @pl.loop(1, count)
    def _(step):
        copy_to(lax.rem(me + step, count)).start()

    own = pltpu.make_async_copy(arrival_ref.at[p, :, mine], out_ref.at[:, columns(p)], local_sems.at[0])
    kept = pltpu.make_async_copy(send_ref.at[me], recv_ref.at[me], local_sems.at[1])
    own.start()
    kept.start()
    own.wait()
    kept.wait()

    @pl.loop(1, count)
    def _(step):
        peer = lax.rem(me + step, count)
        copy_to(peer).wait_send()
        remote(send_ref.at[peer], recv_ref.at[peer], send_sems.at[peer], recv_sems.at[peer], peer).wait_recv()

    for o in range(1, SLAB):
        q = (p + o) % SLAB
        block(o).wait_send()
        remote(
            arrival_ref.at[q, :, mine], out_ref.at[:, columns(q)],
            slab_send.at[o - 1], slab_recv.at[q], base + q,
        ).wait_recv()


def on_device(slowness, ocean, start_times, source_cells, gauge_cells, gauge_owner):
    index = lax.axis_index("space")
    count = lax.axis_size("space")
    rows, width = slowness.shape
    sources = start_times.shape[0]
    gauges = gauge_cells.shape[0]
    size = width // SLAB
    window = size + 2 * LANES
    half = window // 2
    phases = half // LANES
    f32 = jnp.float32
    high = rows * SLAB + 2 * HALO
    far = jnp.float32(far_value)
    q = index % SLAB
    slab = index // SLAB
    left = window_start(q, size)

    cost = jnp.where(ocean == 1, slowness, jnp.float32(land_cost))
    info = jnp.stack([gauge_cells, gauge_owner[:, 0]])[:, None, :]
    first = (slab * (SLAB * rows * width) + left).astype(jnp.int32).reshape(1)
    dma = pltpu.SemaphoreType.DMA

    times, packed, g4 = pl.pallas_call(
        functools.partial(gather, count),
        out_shape=(
            jax.ShapeDtypeStruct((SLAB * rows * phases * SUBS, LANES), f32),
            jax.ShapeDtypeStruct((high * phases * SUBS, LANES), f32),
            jax.ShapeDtypeStruct((SLAB,) + info.shape, jnp.int32),
        ),
        in_specs=[SMEM, SMEM, ANY, ANY, ANY],
        out_specs=(VMEM, VMEM, ANY),
        scratch_shapes=[
            pltpu.VMEM((half, half), f32),
            pltpu.VMEM((SLAB, sources, rows, window), f32),
            pltpu.VMEM((SLAB, rows, window), f32),
            pltpu.VMEM((rows, window), f32),
            pltpu.VMEM((rows, window), f32),
            dma((3,)), dma((SLAB - 1, 3)), dma((SLAB, 3)), dma((2,)), dma((2,)),
        ],
        compiler_params=pltpu.CompilerParams(
            collective_id=0, has_side_effects=True, vmem_limit_bytes=48 * 1024 * 1024
        ),
        name="gather",
    )(first, source_cells, start_times, cost, info)

    grid = (SLAB * rows, phases, SUBS, LANES)
    edged = (phases + 4, SUBS, LANES)
    times = pl.pallas_call(
        functools.partial(march, count),
        out_shape=jax.ShapeDtypeStruct(grid, f32),
        in_specs=[VMEM, VMEM],
        out_specs=VMEM,
        scratch_shapes=[
            pltpu.VMEM((high,) + edged, f32),
            pltpu.VMEM((high,) + edged, f32),
            pltpu.VMEM((2, HALO) + edged, f32),
            pltpu.VMEM((BLOCKS, 2, HALO) + edged, f32),
            dma((BLOCKS, 2)), dma((BLOCKS, 2)),
        ],
        compiler_params=pltpu.CompilerParams(
            collective_id=1, has_side_effects=True, vmem_limit_bytes=48 * 1024 * 1024
        ),
        name="march",
    )(times.reshape(grid), packed.reshape((high,) + grid[1:]))

    cells, owners = g4[:, 0, 0], g4[:, 1, 0]
    column = cells % width
    inside = column // size == q
    local = jnp.clip(column - left, 0, window - 1)
    where = local % half
    grid_row = jnp.arange(SLAB, dtype=jnp.int32)[:, None] * rows + cells // width
    spots = (grid_row * phases + where % phases) * SUBS
    turns = (jnp.arange(gauges, dtype=jnp.int32)[None, :] - where // phases) % LANES
    arrival, lines = pl.pallas_call(
        finish,
        out_shape=(
            jax.ShapeDtypeStruct((SLAB, rows, window), f32),
            jax.ShapeDtypeStruct((SLAB, SUBS, gauges), f32),
        ),
        in_specs=[SMEM, SMEM, VMEM],
        out_specs=(VMEM, VMEM),
        scratch_shapes=[
            pltpu.VMEM((SLAB * rows * phases * SUBS, LANES), f32),
            pltpu.VMEM((half, half), f32),
        ],
        compiler_params=PARAMS,
        name="finish",
    )(spots.reshape(-1), turns.reshape(-1), times.reshape(-1, LANES))

    lines = lines.reshape(SLAB, sources, 2, gauges)
    values = jnp.where((local // half == 0)[:, None, :], lines[:, :, 0], lines[:, :, 1])
    values = jnp.minimum(values, jnp.float32(clip_value)) / clip_value
    values = jnp.where(inside[:, None, :], values, 0.0)
    capacity = max(2, 2 * gauges // count)
    slots = jnp.arange(count * capacity, dtype=jnp.int32)
    same = (owners[:, :, None] == owners[:, None, :]) & (
        jnp.arange(gauges)[None, :] < jnp.arange(gauges)[:, None]
    )
    ranks = jnp.sum(same.astype(jnp.int32), axis=2)
    target = owners * capacity + ranks
    placing = (target[:, :, None] == slots[None, None, :]).astype(f32)
    placed = jnp.einsum(
        "bsg,bgt->bst", values, placing,
        precision=lax.Precision.HIGHEST, preferred_element_type=f32,
    )
    amount = SLAB * sources * capacity
    lanes = -(-amount // LANES) * LANES
    placed = placed.reshape(SLAB, sources, count, capacity).transpose(2, 0, 1, 3)
    placed = jnp.pad(placed.reshape(count, 1, amount), ((0, 0), (0, 0), (0, lanes - amount)))
    arrival, received = pl.pallas_call(
        functools.partial(deliver, count, size),
        out_shape=(jax.ShapeDtypeStruct((rows, width), f32), jax.ShapeDtypeStruct(placed.shape, f32)),
        in_specs=[VMEM, VMEM],
        out_specs=(VMEM, VMEM),
        scratch_shapes=[dma((count,)), dma((count,)), dma((SLAB - 1,)), dma((SLAB,)), dma((2,))],
        compiler_params=pltpu.CompilerParams(collective_id=BLOCKS, has_side_effects=True),
        name="deliver",
    )(arrival, placed)
    received = received[:, 0, :amount].reshape(count // SLAB, SLAB, SLAB, sources, capacity)
    received = jnp.sum(received, axis=1).transpose(2, 0, 1, 3)
    return (arrival, received.reshape(1, sources, count * capacity))


def solution(mesh):
    return jax.shard_map(
        on_device,
        mesh=mesh,
        in_specs=(
            P(("groups", "space"), None),
            P(("groups", "space"), None),
            P("groups", "space", None),
            P("groups"),
            P(("groups", "space")),
            P(("groups", "space"), None),
        ),
        out_specs=(P(("groups", "space"), None), P(("groups", "space"), None, None)),
        check_vma=False,
    )
```

```python
import functools

import jax
import jax.numpy as jnp
from jax import lax
from jax.experimental import pallas as pl
from jax.experimental.pallas import tpu as pltpu
from jax.sharding import PartitionSpec as P

SWEEPS = 8
BLOCKS = 3
HALO = 2 * SWEEPS
SLAB = 4

far_value = 1000000.0
land_cost = 10000.0
clip_value = 48.0
root_two = 1.41421356
root_five = 2.23606798

LANES = 128
SUBS = 8
GROUP = 8
EDGE = 4
UNROLL = 32
VMEM = pl.BlockSpec(memory_space=pltpu.VMEM)
SMEM = pl.BlockSpec(memory_space=pltpu.SMEM)
ANY = pl.BlockSpec(memory_space=pl.ANY)
PARAMS = pltpu.CompilerParams(vmem_limit_bytes=48 * 1024 * 1024)
MESH = pl.DeviceIdType.MESH


def window_start(quarter, size):
    return quarter * size - LANES * ((quarter + 2) // 3 + quarter // 3)


def remote(src, dst, send_sem, recv_sem, device):
    return pltpu.make_async_remote_copy(
        src_ref=src,
        dst_ref=dst,
        send_sem=send_sem,
        recv_sem=recv_sem,
        device_id={"space": device},
        device_id_type=MESH,
    )


def signal(barrier, device):
    pl.semaphore_signal(barrier, inc=1, device_id={"space": device}, device_id_type=MESH)


def ends(me, count):
    slab = me // SLAB
    return slab > 0, slab < count // SLAB - 1


def greet(barrier, me, count):
    below, above = ends(me, count)

    @pl.when(below)
    def _():
        signal(barrier, me - SLAB)

    @pl.when(above)
    def _():
        signal(barrier, me + SLAB)

    return below, above


def meet(barrier, me, count, others):
    slabs = count // SLAB
    slab = me // SLAB
    below = (slab + slabs - 1) // slabs
    above = (2 * slabs - 2 - slab) // slabs
    pl.semaphore_wait(barrier, others + below + above)


def selection(phases, back):
    size = phases * LANES
    packed = lax.broadcasted_iota(jnp.int32, (size, size), 0 if back else 1)
    plain = lax.broadcasted_iota(jnp.int32, (size, size), 1 if back else 0)
    return jnp.where(plain == packed % LANES * phases + packed // LANES, 1.0, 0.0)


def gather(count, first_ref, cells_ref, start_ref, cost_ref, info_ref, times_ref, packed_ref, g_ref,
           choose, t_ref, c_ref, pc, nc, local_sems, send_sems, recv_sems, far_send, far_recv):
    me = lax.axis_index("space")
    base = me // SLAB * SLAB
    p = me % SLAB
    _, sources, rows, window = t_ref.shape
    width = start_ref.shape[2]
    size = width // SLAB
    barrier = pltpu.get_barrier_semaphore()
    for o in range(1, SLAB):
        signal(barrier, base + (p + o) % SLAB)
    below, above = greet(barrier, me, count)
    meet(barrier, me, count, SLAB - 1)
    kinds = (c_ref, g_ref, t_ref)

    def piece(q, n):
        cols = pl.ds(pl.multiple_of(window_start(q, size), LANES), window)
        return (cost_ref.at[:, cols], info_ref, start_ref.at[:, :, cols])[n], kinds[n].at[p]

    def outgoing(o, n):
        q = (p + o) % SLAB
        return remote(*piece(q, n), send_sems.at[o - 1, n], recv_sems.at[p, n], base + q)

    def arrived(o, n):
        q = (p + o) % SLAB
        ref = kinds[n].at[q]
        remote(ref, ref, send_sems.at[o - 1, n], recv_sems.at[q, n], base + q).wait_recv()

    local = [pltpu.make_async_copy(*piece(p, n), local_sems.at[n]) for n in range(3)]
    for n in range(3):
        for o in (2, 1, 3):
            outgoing(o, n).start()
        local[n].start()
    half = window // 2
    phases = half // LANES
    choose[...] = selection(phases, False)
    row = lax.broadcasted_iota(jnp.int32, (rows, half), 0)
    col = lax.broadcasted_iota(jnp.int32, (rows, half), 1)
    place = row * width + col
    far = jnp.float32(far_value)
    chunk = rows * phases * SUBS

    def arrange(x):
        return jnp.dot(
            x, choose[...], precision=lax.Precision.HIGHEST, preferred_element_type=jnp.float32
        )

    def put(ref, start, n, y):
        for k in range(phases):
            ref[pl.ds(start + k * SUBS + n, rows, stride=phases * SUBS), :] = y[:, k * LANES : (k + 1) * LANES]

    def pack_times(q):
        for h in range(2):
            cols = slice(h * half, (h + 1) * half)
            xs = []
            for s in range(sources):
                offset = cells_ref[s] - (first_ref[0] + q * (rows * width) + h * half)
                xs.append(jnp.where(place == offset, 0.0, t_ref[q, s, :, cols]))
            y = arrange(jnp.concatenate(xs, axis=0))
            for s in range(sources):
                put(times_ref, q * chunk, s * 2 + h, y[s * rows : (s + 1) * rows])

    def pack_costs(xs, starts):
        for h in range(2):
            y = arrange(jnp.concatenate([x[:, h * half : (h + 1) * half] for x in xs], axis=0))
            for n, start in enumerate(starts):
                for s in range(sources):
                    put(packed_ref, start, s * 2 + h, y[n * rows : (n + 1) * rows])

    local[2].wait()
    pack_times(p)
    local[0].wait()
    local[1].wait()
    for o in range(1, SLAB):
        arrived(o, 0)
        arrived(o, 1)

    def lower():
        return remote(c_ref.at[0], nc, far_send.at[0], far_recv.at[0], me - SLAB)

    def upper():
        return remote(c_ref.at[SLAB - 1], pc, far_send.at[1], far_recv.at[1], me + SLAB)

    @pl.when(below)
    def _():
        lower().start()

    @pl.when(above)
    def _():
        upper().start()

    pack_costs([c_ref[q] for q in range(SLAB)], [(q + 1) * chunk for q in range(SLAB)])

    @pl.when(below)
    def _():
        lower().wait_send()
        remote(pc, pc, far_send.at[1], far_recv.at[1], me - SLAB).wait_recv()

    @pl.when(above)
    def _():
        upper().wait_send()
        remote(nc, nc, far_send.at[0], far_recv.at[0], me + SLAB).wait_recv()

    pack_costs(
        [jnp.where(below, pc[...], far), jnp.where(above, nc[...], far)], [0, (SLAB + 1) * chunk]
    )
    for o in (1, 3, 2):
        arrived(o, 2)
        pack_times((p + o) % SLAB)
    for o in range(1, SLAB):
        for n in range(3):
            outgoing(o, n).wait_send()


def edge_fixers():
    sub = lax.broadcasted_iota(jnp.int32, (SUBS, LANES), 0)
    lane = lax.broadcasted_iota(jnp.int32, (SUBS, LANES), 1)
    far = jnp.float32(far_value)

    def from_left(x):
        y = pltpu.roll(x, 1, 1)
        z = jnp.where(sub % 2 == 0, far, pltpu.roll(y, 1, 0))
        return jnp.where(lane == 0, z, y)

    def from_right(x):
        y = pltpu.roll(x, LANES - 1, 1)
        z = jnp.where(sub % 2 == 1, far, pltpu.roll(y, SUBS - 1, 0))
        return jnp.where(lane == LANES - 1, z, y)

    return from_left, from_right


def march(count, times_ref, cost_ref, out_ref, one, two, one_edge, two_edge, staged, landed,
          send_sems, recv_sems):
    me = lax.axis_index("space")
    barrier = pltpu.get_barrier_semaphore()
    below, above = greet(barrier, me, count)
    rows, phases = times_ref.shape[0], times_ref.shape[1]
    high = cost_ref.shape[0]
    total = phases + 4
    far = jnp.float32(far_value)
    from_left, from_right = edge_fixers()
    first, second = (one, one_edge), (two, two_edge)

    def edges(field, start, size):
        body, edge = field
        for i in range(size):
            r = start + i
            edge[r, 0] = from_left(body[r, phases - 2])
            edge[r, 1] = from_left(body[r, phases - 1])
            edge[r, 2] = from_right(body[r, 0])
            edge[r, 3] = from_right(body[r, 1])

    def enter(r, vals):
        for k in range(phases):
            one[r, k] = vals[k]
        one_edge[r, 0] = from_left(vals[phases - 2])
        one_edge[r, 1] = from_left(vals[phases - 1])
        one_edge[r, 2] = from_right(vals[0])
        one_edge[r, 3] = from_right(vals[1])

    @pl.loop(0, rows // 8)
    def _(g):
        for i in range(8):
            enter(HALO + 8 * g + i, [times_ref[8 * g + i, k] for k in range(phases)])

    meet(barrier, me, count, 0)

    def relax(src, dst, r0, size):
        body, edge = src
        t = {}

        def value(r, x):
            if x < 2:
                return edge[r, x]
            return edge[r, x - phases] if x >= phases + 2 else body[r, x - 2]

        def load(d):
            inner = range(1, total - 1) if d in (-2, size + 1) else range(total)
            t[d] = {x: value(r0 + d, x) for x in inner}

        for d in (-2, -1, 0, 1):
            load(d)
        for i in range(size):
            load(i + 2)
            r = r0 + i
            m = t[i]
            a = [jnp.minimum(t[i - 1][x], t[i + 1][x]) for x in range(total)]
            b = {x: jnp.minimum(t[i - 2][x], t[i + 2][x]) for x in range(1, total - 1)}
            for k in range(2, phases + 2):
                c = cost_ref[r, k - 2]
                near = jnp.minimum(a[k], jnp.minimum(m[k - 1], m[k + 1]))
                diag = jnp.minimum(a[k - 1], a[k + 1])
                knight = jnp.minimum(
                    jnp.minimum(a[k - 2], a[k + 2]), jnp.minimum(b[k - 1], b[k + 1])
                )
                best = jnp.minimum(near + c, diag + c * root_two)
                best = jnp.minimum(best, knight + c * root_five)
                dst[0][r, k - 2] = jnp.minimum(m[k], best)

    def sweep(src, dst, starts, length, size):
        groups = (length + size - 1) // size

        def offset(group):
            return jnp.minimum(size * group, length - size)

        @pl.loop(0, groups)
        def _(group):
            for start in starts:
                edges(dst, start + offset(jnp.maximum(group - 1, 0)), size)
            for start in starts:
                relax(src, dst, start + offset(group), size)

        for start in starts:
            edges(dst, start + offset(groups - 1), size)

    def inner(src, dst, j):
        sweep(src, dst, [HALO + 4 * j], rows - 8 * j, GROUP)

    def outer(src, dst, j):
        sweep(src, dst, [2 * j, high - HALO - 4 * j], HALO + 2 * j, EDGE)

    last = (rows - GROUP) // 8

    @pl.loop(0, BLOCKS)
    def _(block):
        def down():
            return remote(staged.at[0], landed.at[block, 1], send_sems.at[block, 0],
                          recv_sems.at[block, 1], me - SLAB)

        def up():
            return remote(staged.at[1], landed.at[block, 0], send_sems.at[block, 1],
                          recv_sems.at[block, 0], me + SLAB)

        @pl.loop(0, HALO // 4)
        def _(g):
            for i in range(4):
                r = 4 * g + i
                for k in range(phases):
                    staged[0, r, k] = one[HALO + r, k]
                    staged[1, r, k] = one[high - 2 * HALO + r, k]

        @pl.when(below)
        def _():
            down().start()

        @pl.when(above)
        def _():
            up().start()

        inner_pairs = min(SWEEPS, last) // 2

        @pl.loop(0, inner_pairs)
        def _(step):
            inner(first, second, 2 * step + 1)
            inner(second, first, 2 * step + 2)

        for j in range(2 * inner_pairs + 1, min(SWEEPS, last) + 1):
            inner(first, second, j)

        @pl.when(below)
        def _():
            down().wait_send()
            remote(landed.at[block, 0], landed.at[block, 0], send_sems.at[block, 0],
                   recv_sems.at[block, 0], me - SLAB).wait_recv()

        @pl.when(above)
        def _():
            up().wait_send()
            remote(landed.at[block, 1], landed.at[block, 1], send_sems.at[block, 1],
                   recv_sems.at[block, 1], me + SLAB).wait_recv()

        @pl.loop(0, HALO // 4)
        def _(g):
            for i in range(4):
                r = 4 * g + i
                enter(r, [jnp.where(below, landed[block, 0, r, k], far) for k in range(phases)])
                enter(
                    high - HALO + r,
                    [jnp.where(above, landed[block, 1, r, k], far) for k in range(phases)],
                )

        @pl.loop(0, SWEEPS // 2)
        def _(step):
            outer(first, second, 2 * step + 1)
            outer(second, first, 2 * step + 2)

    @pl.loop(0, rows // 8)
    def _(g):
        for i in range(8):
            for k in range(phases):
                out_ref[8 * g + i, k] = one[HALO + 8 * g + i, k]


def finish(spots_ref, turns_ref, times_ref, arrival_ref, gauge_ref, least, choose):
    slab, rows, window = arrival_ref.shape
    half = window // 2
    phases = half // LANES
    choose[...] = selection(phases, True)
    steps = slab * rows * phases
    lane = lax.broadcasted_iota(jnp.int32, (SUBS, LANES), 1)

    @pl.loop(0, steps // UNROLL)
    def _(group):
        for i in range(UNROLL):
            row = pl.ds(pl.multiple_of((group * UNROLL + i) * SUBS, SUBS), SUBS)
            x = times_ref[row, :]
            x = jnp.minimum(x, pltpu.roll(x, 2, 0))
            least[row, :] = jnp.minimum(x, pltpu.roll(x, 4, 0))

    for h in range(2):
        x = jnp.concatenate(
            [least[pl.ds(k * SUBS + h, slab * rows, stride=phases * SUBS), :] for k in range(phases)],
            axis=1,
        )
        x = jnp.minimum(x, clip_value) / clip_value
        y = jnp.dot(x, choose[...], precision=lax.Precision.HIGHEST, preferred_element_type=jnp.float32)
        for b in range(slab):
            arrival_ref[b, :, h * half : (h + 1) * half] = y[b * rows : (b + 1) * rows]

    gauges = gauge_ref.shape[2]
    for b in range(slab):
        for start in range(0, gauges, LANES):

            def step(group, acc):
                for i in range(UNROLL):
                    n = group * UNROLL + i
                    g = b * gauges + start + n
                    x = times_ref[pl.ds(pl.multiple_of(spots_ref[g], SUBS), SUBS), :]
                    x = pltpu.roll(x, turns_ref[g], 1)
                    acc = jnp.where(lane == n, x, acc)
                return acc

            acc = lax.fori_loop(0, LANES // UNROLL, step, jnp.zeros((SUBS, LANES), jnp.float32))
            gauge_ref[b, :, start : start + LANES] = acc


def deliver(count, size, arrival_ref, send_ref, out_ref, recv_ref, send_sems, recv_sems,
            slab_send, slab_recv, local_sems):
    me = lax.axis_index("space")
    base = me // SLAB * SLAB
    p = me % SLAB
    barrier = pltpu.get_barrier_semaphore()

    @pl.loop(1, count)
    def _(step):
        signal(barrier, lax.rem(me + step, count))

    pl.semaphore_wait(barrier, count - 1)
    mine = pl.ds(pl.multiple_of(p * size - window_start(p, size), LANES), size)

    def columns(q):
        return pl.ds(pl.multiple_of(q * size, LANES), size)

    def block(o):
        q = (p + o) % SLAB
        return remote(
            arrival_ref.at[q, :, mine], out_ref.at[:, columns(p)],
            slab_send.at[o - 1], slab_recv.at[p], base + q,
        )

    def copy_to(peer):
        return remote(send_ref.at[peer], recv_ref.at[me], send_sems.at[peer], recv_sems.at[me], peer)

    for o in (2, 1, 3):
        block(o).start()

    @pl.loop(1, count)
    def _(step):
        copy_to(lax.rem(me + step, count)).start()

    own = pltpu.make_async_copy(arrival_ref.at[p, :, mine], out_ref.at[:, columns(p)], local_sems.at[0])
    kept = pltpu.make_async_copy(send_ref.at[me], recv_ref.at[me], local_sems.at[1])
    own.start()
    kept.start()
    own.wait()
    kept.wait()

    @pl.loop(1, count)
    def _(step):
        peer = lax.rem(me + step, count)
        copy_to(peer).wait_send()
        remote(send_ref.at[peer], recv_ref.at[peer], send_sems.at[peer], recv_sems.at[peer], peer).wait_recv()

    for o in range(1, SLAB):
        q = (p + o) % SLAB
        block(o).wait_send()
        remote(
            arrival_ref.at[q, :, mine], out_ref.at[:, columns(q)],
            slab_send.at[o - 1], slab_recv.at[q], base + q,
        ).wait_recv()


def on_device(slowness, ocean, start_times, source_cells, gauge_cells, gauge_owner):
    index = lax.axis_index("space")
    count = lax.axis_size("space")
    rows, width = slowness.shape
    sources = start_times.shape[0]
    gauges = gauge_cells.shape[0]
    size = width // SLAB
    window = size + 2 * LANES
    half = window // 2
    phases = half // LANES
    f32 = jnp.float32
    high = rows * SLAB + 2 * HALO
    far = jnp.float32(far_value)
    q = index % SLAB
    slab = index // SLAB
    left = window_start(q, size)

    cost = jnp.where(ocean == 1, slowness, jnp.float32(land_cost))
    info = jnp.stack([gauge_cells, gauge_owner[:, 0]])[:, None, :]
    first = (slab * (SLAB * rows * width) + left).astype(jnp.int32).reshape(1)
    dma = pltpu.SemaphoreType.DMA

    times, packed, g4 = pl.pallas_call(
        functools.partial(gather, count),
        out_shape=(
            jax.ShapeDtypeStruct((SLAB * rows * phases * SUBS, LANES), f32),
            jax.ShapeDtypeStruct((high * phases * SUBS, LANES), f32),
            jax.ShapeDtypeStruct((SLAB,) + info.shape, jnp.int32),
        ),
        in_specs=[SMEM, SMEM, ANY, ANY, ANY],
        out_specs=(VMEM, VMEM, ANY),
        scratch_shapes=[
            pltpu.VMEM((half, half), f32),
            pltpu.VMEM((SLAB, sources, rows, window), f32),
            pltpu.VMEM((SLAB, rows, window), f32),
            pltpu.VMEM((rows, window), f32),
            pltpu.VMEM((rows, window), f32),
            dma((3,)), dma((SLAB - 1, 3)), dma((SLAB, 3)), dma((2,)), dma((2,)),
        ],
        compiler_params=pltpu.CompilerParams(
            collective_id=0, has_side_effects=True, vmem_limit_bytes=48 * 1024 * 1024
        ),
        name="gather",
    )(first, source_cells, start_times, cost, info)

    grid = (SLAB * rows, phases, SUBS, LANES)
    edge = (4, SUBS, LANES)
    times = pl.pallas_call(
        functools.partial(march, count),
        out_shape=jax.ShapeDtypeStruct(grid, f32),
        in_specs=[VMEM, VMEM],
        out_specs=VMEM,
        scratch_shapes=[
            pltpu.VMEM((high,) + grid[1:], f32),
            pltpu.VMEM((high,) + grid[1:], f32),
            pltpu.VMEM((high,) + edge, f32),
            pltpu.VMEM((high,) + edge, f32),
            pltpu.VMEM((2, HALO) + grid[1:], f32),
            pltpu.VMEM((BLOCKS, 2, HALO) + grid[1:], f32),
            dma((BLOCKS, 2)), dma((BLOCKS, 2)),
        ],
        compiler_params=pltpu.CompilerParams(
            collective_id=1, has_side_effects=True, vmem_limit_bytes=48 * 1024 * 1024
        ),
        name="march",
    )(times.reshape(grid), packed.reshape((high,) + grid[1:]))

    cells, owners = g4[:, 0, 0], g4[:, 1, 0]
    column = cells % width
    inside = column // size == q
    local = jnp.clip(column - left, 0, window - 1)
    where = local % half
    grid_row = jnp.arange(SLAB, dtype=jnp.int32)[:, None] * rows + cells // width
    spots = (grid_row * phases + where % phases) * SUBS
    turns = (jnp.arange(gauges, dtype=jnp.int32)[None, :] - where // phases) % LANES
    arrival, lines = pl.pallas_call(
        finish,
        out_shape=(
            jax.ShapeDtypeStruct((SLAB, rows, window), f32),
            jax.ShapeDtypeStruct((SLAB, SUBS, gauges), f32),
        ),
        in_specs=[SMEM, SMEM, VMEM],
        out_specs=(VMEM, VMEM),
        scratch_shapes=[
            pltpu.VMEM((SLAB * rows * phases * SUBS, LANES), f32),
            pltpu.VMEM((half, half), f32),
        ],
        compiler_params=PARAMS,
        name="finish",
    )(spots.reshape(-1), turns.reshape(-1), times.reshape(-1, LANES))

    lines = lines.reshape(SLAB, sources, 2, gauges)
    values = jnp.where((local // half == 0)[:, None, :], lines[:, :, 0], lines[:, :, 1])
    values = jnp.minimum(values, jnp.float32(clip_value)) / clip_value
    values = jnp.where(inside[:, None, :], values, 0.0)
    capacity = max(2, 2 * gauges // count)
    slots = jnp.arange(count * capacity, dtype=jnp.int32)
    same = (owners[:, :, None] == owners[:, None, :]) & (
        jnp.arange(gauges)[None, :] < jnp.arange(gauges)[:, None]
    )
    ranks = jnp.sum(same.astype(jnp.int32), axis=2)
    target = owners * capacity + ranks
    placing = (target[:, :, None] == slots[None, None, :]).astype(f32)
    placed = jnp.einsum(
        "bsg,bgt->bst", values, placing,
        precision=lax.Precision.HIGHEST, preferred_element_type=f32,
    )
    amount = SLAB * sources * capacity
    lanes = -(-amount // LANES) * LANES
    placed = placed.reshape(SLAB, sources, count, capacity).transpose(2, 0, 1, 3)
    placed = jnp.pad(placed.reshape(count, 1, amount), ((0, 0), (0, 0), (0, lanes - amount)))
    arrival, received = pl.pallas_call(
        functools.partial(deliver, count, size),
        out_shape=(jax.ShapeDtypeStruct((rows, width), f32), jax.ShapeDtypeStruct(placed.shape, f32)),
        in_specs=[VMEM, VMEM],
        out_specs=(VMEM, VMEM),
        scratch_shapes=[dma((count,)), dma((count,)), dma((SLAB - 1,)), dma((SLAB,)), dma((2,))],
        compiler_params=pltpu.CompilerParams(collective_id=BLOCKS, has_side_effects=True),
        name="deliver",
    )(arrival, placed)
    received = received[:, 0, :amount].reshape(count // SLAB, SLAB, SLAB, sources, capacity)
    received = jnp.sum(received, axis=1).transpose(2, 0, 1, 3)
    return (arrival, received.reshape(1, sources, count * capacity))


def solution(mesh):
    return jax.shard_map(
        on_device,
        mesh=mesh,
        in_specs=(
            P(("groups", "space"), None),
            P(("groups", "space"), None),
            P("groups", "space", None),
            P("groups"),
            P(("groups", "space")),
            P(("groups", "space"), None),
        ),
        out_specs=(P(("groups", "space"), None), P(("groups", "space"), None, None)),
        check_vma=False,
    )
```

```python
import functools

import jax
import jax.numpy as jnp
from jax import lax
from jax.experimental import pallas as pl
from jax.experimental.pallas import tpu as pltpu
from jax.sharding import PartitionSpec as P

SWEEPS = 8
BLOCKS = 3
HALO = 2 * SWEEPS
SLAB = 4

far_value = 1000000.0
land_cost = 10000.0
clip_value = 48.0
root_two = 1.41421356
root_five = 2.23606798

LANES = 128
SUBS = 8
GROUP = 8
EDGE = 8
UNROLL = 32
VMEM = pl.BlockSpec(memory_space=pltpu.VMEM)
SMEM = pl.BlockSpec(memory_space=pltpu.SMEM)
ANY = pl.BlockSpec(memory_space=pl.ANY)
HBM = pl.BlockSpec(memory_space=pltpu.HBM)
PARAMS = pltpu.CompilerParams(vmem_limit_bytes=48 * 1024 * 1024)
MESH = pl.DeviceIdType.MESH


def window_start(quarter, size):
    return quarter * size - LANES * ((quarter + 2) // 3 + quarter // 3)


def remote(src, dst, send_sem, recv_sem, device):
    return pltpu.make_async_remote_copy(
        src_ref=src,
        dst_ref=dst,
        send_sem=send_sem,
        recv_sem=recv_sem,
        device_id={"space": device},
        device_id_type=MESH,
    )


def signal(barrier, device):
    pl.semaphore_signal(barrier, inc=1, device_id={"space": device}, device_id_type=MESH)


def ends(me, count):
    slab = me // SLAB
    return slab > 0, slab < count // SLAB - 1


def greet(barrier, me, count):
    below, above = ends(me, count)

    @pl.when(below)
    def _():
        signal(barrier, me - SLAB)

    @pl.when(above)
    def _():
        signal(barrier, me + SLAB)

    return below, above


def meet(barrier, me, count, others):
    slabs = count // SLAB
    slab = me // SLAB
    below = (slab + slabs - 1) // slabs
    above = (2 * slabs - 2 - slab) // slabs
    pl.semaphore_wait(barrier, others + below + above)


def selection(phases, back):
    size = phases * LANES
    packed = lax.broadcasted_iota(jnp.int32, (size, size), 0 if back else 1)
    plain = lax.broadcasted_iota(jnp.int32, (size, size), 1 if back else 0)
    return jnp.where(plain == packed % LANES * phases + packed // LANES, 1.0, 0.0)


def gather(count, first_ref, cells_ref, start_ref, cost_ref, info_ref, times_ref, packed_ref, g_ref,
           choose, t_ref, c_ref, pc, nc, local_sems, send_sems, recv_sems, far_send, far_recv):
    me = lax.axis_index("space")
    base = me // SLAB * SLAB
    p = me % SLAB
    _, sources, rows, window = t_ref.shape
    width = start_ref.shape[2]
    size = width // SLAB
    barrier = pltpu.get_barrier_semaphore()
    for o in range(1, SLAB):
        signal(barrier, base + (p + o) % SLAB)
    below, above = greet(barrier, me, count)
    meet(barrier, me, count, SLAB - 1)
    kinds = (c_ref, g_ref, t_ref)

    def piece(q, n):
        cols = pl.ds(pl.multiple_of(window_start(q, size), LANES), window)
        return (cost_ref.at[:, cols], info_ref, start_ref.at[:, :, cols])[n], kinds[n].at[p]

    def outgoing(o, n):
        q = (p + o) % SLAB
        return remote(*piece(q, n), send_sems.at[o - 1, n], recv_sems.at[p, n], base + q)

    def arrived(o, n):
        q = (p + o) % SLAB
        ref = kinds[n].at[q]
        remote(ref, ref, send_sems.at[o - 1, n], recv_sems.at[q, n], base + q).wait_recv()

    local = [pltpu.make_async_copy(*piece(p, n), local_sems.at[n]) for n in range(3)]
    for n in range(3):
        for o in (2, 1, 3):
            outgoing(o, n).start()
        local[n].start()
    half = window // 2
    phases = half // LANES
    choose[...] = selection(phases, False)
    row = lax.broadcasted_iota(jnp.int32, (rows, half), 0)
    col = lax.broadcasted_iota(jnp.int32, (rows, half), 1)
    place = row * width + col
    far = jnp.float32(far_value)
    chunk = rows * phases * SUBS

    def arrange(x):
        return jnp.dot(
            x, choose[...], precision=lax.Precision.HIGHEST, preferred_element_type=jnp.float32
        )

    def put(ref, start, n, y):
        for k in range(phases):
            ref[pl.ds(start + k * SUBS + n, rows, stride=phases * SUBS), :] = y[:, k * LANES : (k + 1) * LANES]

    def pack_times(q):
        for h in range(2):
            cols = slice(h * half, (h + 1) * half)
            xs = []
            for s in range(sources):
                offset = cells_ref[s] - (first_ref[0] + q * (rows * width) + h * half)
                xs.append(jnp.where(place == offset, 0.0, t_ref[q, s, :, cols]))
            y = arrange(jnp.concatenate(xs, axis=0))
            for s in range(sources):
                put(times_ref, q * chunk, s * 2 + h, y[s * rows : (s + 1) * rows])

    def pack_costs(xs, starts):
        for h in range(2):
            y = arrange(jnp.concatenate([x[:, h * half : (h + 1) * half] for x in xs], axis=0))
            for n, start in enumerate(starts):
                for s in range(sources):
                    put(packed_ref, start, s * 2 + h, y[n * rows : (n + 1) * rows])

    local[2].wait()
    pack_times(p)
    local[0].wait()
    local[1].wait()
    for o in range(1, SLAB):
        arrived(o, 0)
        arrived(o, 1)

    def lower():
        return remote(c_ref.at[0], nc, far_send.at[0], far_recv.at[0], me - SLAB)

    def upper():
        return remote(c_ref.at[SLAB - 1], pc, far_send.at[1], far_recv.at[1], me + SLAB)

    @pl.when(below)
    def _():
        lower().start()

    @pl.when(above)
    def _():
        upper().start()

    pack_costs([c_ref[q] for q in range(SLAB)], [(q + 1) * chunk for q in range(SLAB)])

    @pl.when(below)
    def _():
        lower().wait_send()
        remote(pc, pc, far_send.at[1], far_recv.at[1], me - SLAB).wait_recv()

    @pl.when(above)
    def _():
        upper().wait_send()
        remote(nc, nc, far_send.at[0], far_recv.at[0], me + SLAB).wait_recv()

    pack_costs(
        [jnp.where(below, pc[...], far), jnp.where(above, nc[...], far)], [0, (SLAB + 1) * chunk]
    )
    for o in (1, 3, 2):
        arrived(o, 2)
        pack_times((p + o) % SLAB)
    for o in range(1, SLAB):
        for n in range(3):
            outgoing(o, n).wait_send()


def edge_fixers():
    sub = lax.broadcasted_iota(jnp.int32, (SUBS, LANES), 0)
    lane = lax.broadcasted_iota(jnp.int32, (SUBS, LANES), 1)
    far = jnp.float32(far_value)

    def from_left(x):
        y = pltpu.roll(x, 1, 1)
        z = jnp.where(sub % 2 == 0, far, pltpu.roll(y, 1, 0))
        return jnp.where(lane == 0, z, y)

    def from_right(x):
        y = pltpu.roll(x, LANES - 1, 1)
        z = jnp.where(sub % 2 == 1, far, pltpu.roll(y, SUBS - 1, 0))
        return jnp.where(lane == LANES - 1, z, y)

    return from_left, from_right


def march(count, times_ref, cost_ref, out_ref, one, two, one_edge, two_edge, staged, landed,
          send_sems, recv_sems):
    me = lax.axis_index("space")
    barrier = pltpu.get_barrier_semaphore()
    below, above = greet(barrier, me, count)
    rows, phases = times_ref.shape[0], times_ref.shape[1]
    high = cost_ref.shape[0]
    total = phases + 4
    far = jnp.float32(far_value)
    from_left, from_right = edge_fixers()
    first, second = (one, one_edge), (two, two_edge)

    def edges(field, start, size):
        body, edge = field
        for i in range(size):
            r = start + i
            edge[r, 0] = from_left(body[r, phases - 2])
            edge[r, 1] = from_left(body[r, phases - 1])
            edge[r, 2] = from_right(body[r, 0])
            edge[r, 3] = from_right(body[r, 1])

    def enter(r, vals):
        for k in range(phases):
            one[r, k] = vals[k]
        one_edge[r, 0] = from_left(vals[phases - 2])
        one_edge[r, 1] = from_left(vals[phases - 1])
        one_edge[r, 2] = from_right(vals[0])
        one_edge[r, 3] = from_right(vals[1])

    @pl.loop(0, rows // 8)
    def _(g):
        for i in range(8):
            enter(HALO + 8 * g + i, [times_ref[8 * g + i, k] for k in range(phases)])

    meet(barrier, me, count, 0)

    def relax(src, dst, r0, size):
        body, edge = src
        t = {}

        def value(r, x):
            if x < 2:
                return edge[r, x]
            return edge[r, x - phases] if x >= phases + 2 else body[r, x - 2]

        def load(d):
            inner = range(1, total - 1) if d in (-2, size + 1) else range(total)
            t[d] = {x: value(r0 + d, x) for x in inner}

        for d in (-2, -1, 0, 1):
            load(d)
        for i in range(size):
            load(i + 2)
            r = r0 + i
            m = t[i]
            a = [jnp.minimum(t[i - 1][x], t[i + 1][x]) for x in range(total)]
            b = {x: jnp.minimum(t[i - 2][x], t[i + 2][x]) for x in range(1, total - 1)}
            for k in range(2, phases + 2):
                c = cost_ref[r, k - 2]
                near = jnp.minimum(a[k], jnp.minimum(m[k - 1], m[k + 1]))
                diag = jnp.minimum(a[k - 1], a[k + 1])
                knight = jnp.minimum(
                    jnp.minimum(a[k - 2], a[k + 2]), jnp.minimum(b[k - 1], b[k + 1])
                )
                best = jnp.minimum(near + c, diag + c * root_two)
                best = jnp.minimum(best, knight + c * root_five)
                dst[0][r, k - 2] = jnp.minimum(m[k], best)

    def sweep(src, dst, starts, length, size):
        groups = (length + size - 1) // size

        def offset(group):
            return jnp.minimum(size * group, length - size)

        @pl.loop(0, groups)
        def _(group):
            for start in starts:
                edges(dst, start + offset(jnp.maximum(group - 1, 0)), size)
            for start in starts:
                relax(src, dst, start + offset(group), size)

        for start in starts:
            edges(dst, start + offset(groups - 1), size)

    def inner(src, dst, j):
        sweep(src, dst, [HALO + 4 * j], rows - 8 * j, GROUP)

    def outer(src, dst, j):
        sweep(src, dst, [2 * j, high - HALO - 4 * j], HALO + 2 * j, EDGE)

    last = (rows - GROUP) // 8

    @pl.loop(0, BLOCKS)
    def _(block):
        def down():
            return remote(staged.at[0], landed.at[block, 1], send_sems.at[block, 0],
                          recv_sems.at[block, 1], me - SLAB)

        def up():
            return remote(staged.at[1], landed.at[block, 0], send_sems.at[block, 1],
                          recv_sems.at[block, 0], me + SLAB)

        @pl.loop(0, HALO // 4)
        def _(g):
            for i in range(4):
                r = 4 * g + i
                for k in range(phases):
                    staged[0, r, k] = one[HALO + r, k]
                    staged[1, r, k] = one[high - 2 * HALO + r, k]

        @pl.when(below)
        def _():
            down().start()

        @pl.when(above)
        def _():
            up().start()

        inner_pairs = min(SWEEPS, last) // 2

        @pl.loop(0, inner_pairs)
        def _(step):
            inner(first, second, 2 * step + 1)
            inner(second, first, 2 * step + 2)

        for j in range(2 * inner_pairs + 1, min(SWEEPS, last) + 1):
            inner(first, second, j)

        @pl.when(below)
        def _():
            down().wait_send()
            remote(landed.at[block, 0], landed.at[block, 0], send_sems.at[block, 0],
                   recv_sems.at[block, 0], me - SLAB).wait_recv()

        @pl.when(above)
        def _():
            up().wait_send()
            remote(landed.at[block, 1], landed.at[block, 1], send_sems.at[block, 1],
                   recv_sems.at[block, 1], me + SLAB).wait_recv()

        @pl.loop(0, HALO // 4)
        def _(g):
            for i in range(4):
                r = 4 * g + i
                enter(r, [jnp.where(below, landed[block, 0, r, k], far) for k in range(phases)])
                enter(
                    high - HALO + r,
                    [jnp.where(above, landed[block, 1, r, k], far) for k in range(phases)],
                )

        @pl.loop(0, SWEEPS // 2)
        def _(step):
            outer(first, second, 2 * step + 1)
            outer(second, first, 2 * step + 2)

    @pl.loop(0, rows // 8)
    def _(g):
        for i in range(8):
            for k in range(phases):
                out_ref[8 * g + i, k] = one[HALO + 8 * g + i, k]


def finish(spots_ref, turns_ref, times_ref, arrival_ref, gauge_ref, least, choose):
    slab, rows, window = arrival_ref.shape
    half = window // 2
    phases = half // LANES
    choose[...] = selection(phases, True)
    steps = slab * rows * phases
    lane = lax.broadcasted_iota(jnp.int32, (SUBS, LANES), 1)

    @pl.loop(0, steps // UNROLL)
    def _(group):
        for i in range(UNROLL):
            row = pl.ds(pl.multiple_of((group * UNROLL + i) * SUBS, SUBS), SUBS)
            x = times_ref[row, :]
            x = jnp.minimum(x, pltpu.roll(x, 2, 0))
            least[row, :] = jnp.minimum(x, pltpu.roll(x, 4, 0))

    for h in range(2):
        x = jnp.concatenate(
            [least[pl.ds(k * SUBS + h, slab * rows, stride=phases * SUBS), :] for k in range(phases)],
            axis=1,
        )
        x = jnp.minimum(x, clip_value) / clip_value
        y = jnp.dot(x, choose[...], precision=lax.Precision.HIGHEST, preferred_element_type=jnp.float32)
        for b in range(slab):
            arrival_ref[b, :, h * half : (h + 1) * half] = y[b * rows : (b + 1) * rows]

    gauges = gauge_ref.shape[2]
    for b in range(slab):
        for start in range(0, gauges, LANES):

            def step(group, acc):
                for i in range(UNROLL):
                    n = group * UNROLL + i
                    g = b * gauges + start + n
                    x = times_ref[pl.ds(pl.multiple_of(spots_ref[g], SUBS), SUBS), :]
                    x = pltpu.roll(x, turns_ref[g], 1)
                    acc = jnp.where(lane == n, x, acc)
                return acc

            acc = lax.fori_loop(0, LANES // UNROLL, step, jnp.zeros((SUBS, LANES), jnp.float32))
            gauge_ref[b, :, start : start + LANES] = acc


def deliver(count, size, arrival_ref, send_ref, out_ref, recv_ref, send_sems, recv_sems,
            slab_send, slab_recv, local_sems):
    me = lax.axis_index("space")
    base = me // SLAB * SLAB
    p = me % SLAB
    barrier = pltpu.get_barrier_semaphore()

    @pl.loop(1, count)
    def _(step):
        signal(barrier, lax.rem(me + step, count))

    pl.semaphore_wait(barrier, count - 1)
    mine = pl.ds(pl.multiple_of(p * size - window_start(p, size), LANES), size)

    def columns(q):
        return pl.ds(pl.multiple_of(q * size, LANES), size)

    def block(o):
        q = (p + o) % SLAB
        return remote(
            arrival_ref.at[q, :, mine], out_ref.at[:, columns(p)],
            slab_send.at[o - 1], slab_recv.at[p], base + q,
        )

    def copy_to(peer):
        return remote(send_ref.at[peer], recv_ref.at[me], send_sems.at[peer], recv_sems.at[me], peer)

    for o in (2, 1, 3):
        block(o).start()

    @pl.loop(1, count)
    def _(step):
        copy_to(lax.rem(me + step, count)).start()

    own = pltpu.make_async_copy(arrival_ref.at[p, :, mine], out_ref.at[:, columns(p)], local_sems.at[0])
    kept = pltpu.make_async_copy(send_ref.at[me], recv_ref.at[me], local_sems.at[1])
    own.start()
    kept.start()
    own.wait()
    kept.wait()

    @pl.loop(1, count)
    def _(step):
        peer = lax.rem(me + step, count)
        copy_to(peer).wait_send()
        remote(send_ref.at[peer], recv_ref.at[peer], send_sems.at[peer], recv_sems.at[peer], peer).wait_recv()

    for o in range(1, SLAB):
        q = (p + o) % SLAB
        block(o).wait_send()
        remote(
            arrival_ref.at[q, :, mine], out_ref.at[:, columns(q)],
            slab_send.at[o - 1], slab_recv.at[q], base + q,
        ).wait_recv()


def on_device(slowness, ocean, start_times, source_cells, gauge_cells, gauge_owner):
    index = lax.axis_index("space")
    count = lax.axis_size("space")
    rows, width = slowness.shape
    sources = start_times.shape[0]
    gauges = gauge_cells.shape[0]
    size = width // SLAB
    window = size + 2 * LANES
    half = window // 2
    phases = half // LANES
    f32 = jnp.float32
    high = rows * SLAB + 2 * HALO
    far = jnp.float32(far_value)
    q = index % SLAB
    slab = index // SLAB
    left = window_start(q, size)

    cost = jnp.where(ocean == 1, slowness, jnp.float32(land_cost))
    info = jnp.stack([gauge_cells, gauge_owner[:, 0]])[:, None, :]
    first = (slab * (SLAB * rows * width) + left).astype(jnp.int32).reshape(1)
    dma = pltpu.SemaphoreType.DMA

    times, packed, g4 = pl.pallas_call(
        functools.partial(gather, count),
        out_shape=(
            jax.ShapeDtypeStruct((SLAB * rows * phases * SUBS, LANES), f32),
            jax.ShapeDtypeStruct((high * phases * SUBS, LANES), f32),
            jax.ShapeDtypeStruct((SLAB,) + info.shape, jnp.int32),
        ),
        in_specs=[SMEM, SMEM, HBM, ANY, ANY],
        out_specs=(VMEM, VMEM, ANY),
        scratch_shapes=[
            pltpu.VMEM((half, half), f32),
            pltpu.VMEM((SLAB, sources, rows, window), f32),
            pltpu.VMEM((SLAB, rows, window), f32),
            pltpu.VMEM((rows, window), f32),
            pltpu.VMEM((rows, window), f32),
            dma((3,)), dma((SLAB - 1, 3)), dma((SLAB, 3)), dma((2,)), dma((2,)),
        ],
        compiler_params=pltpu.CompilerParams(
            collective_id=0, has_side_effects=True, vmem_limit_bytes=48 * 1024 * 1024
        ),
        name="gather",
    )(first, source_cells, start_times, cost, info)

    grid = (SLAB * rows, phases, SUBS, LANES)
    edge = (4, SUBS, LANES)
    times = pl.pallas_call(
        functools.partial(march, count),
        out_shape=jax.ShapeDtypeStruct(grid, f32),
        in_specs=[VMEM, VMEM],
        out_specs=VMEM,
        scratch_shapes=[
            pltpu.VMEM((high,) + grid[1:], f32),
            pltpu.VMEM((high,) + grid[1:], f32),
            pltpu.VMEM((high,) + edge, f32),
            pltpu.VMEM((high,) + edge, f32),
            pltpu.VMEM((2, HALO) + grid[1:], f32),
            pltpu.VMEM((BLOCKS, 2, HALO) + grid[1:], f32),
            dma((BLOCKS, 2)), dma((BLOCKS, 2)),
        ],
        compiler_params=pltpu.CompilerParams(
            collective_id=1, has_side_effects=True, vmem_limit_bytes=48 * 1024 * 1024
        ),
        name="march",
    )(times.reshape(grid), packed.reshape((high,) + grid[1:]))

    cells, owners = g4[:, 0, 0], g4[:, 1, 0]
    column = cells % width
    inside = column // size == q
    local = jnp.clip(column - left, 0, window - 1)
    where = local % half
    grid_row = jnp.arange(SLAB, dtype=jnp.int32)[:, None] * rows + cells // width
    spots = (grid_row * phases + where % phases) * SUBS
    turns = (jnp.arange(gauges, dtype=jnp.int32)[None, :] - where // phases) % LANES
    arrival, lines = pl.pallas_call(
        finish,
        out_shape=(
            jax.ShapeDtypeStruct((SLAB, rows, window), f32),
            jax.ShapeDtypeStruct((SLAB, SUBS, gauges), f32),
        ),
        in_specs=[SMEM, SMEM, VMEM],
        out_specs=(VMEM, VMEM),
        scratch_shapes=[
            pltpu.VMEM((SLAB * rows * phases * SUBS, LANES), f32),
            pltpu.VMEM((half, half), f32),
        ],
        compiler_params=PARAMS,
        name="finish",
    )(spots.reshape(-1), turns.reshape(-1), times.reshape(-1, LANES))

    lines = lines.reshape(SLAB, sources, 2, gauges)
    values = jnp.where((local // half == 0)[:, None, :], lines[:, :, 0], lines[:, :, 1])
    values = jnp.minimum(values, jnp.float32(clip_value)) / clip_value
    values = jnp.where(inside[:, None, :], values, 0.0)
    capacity = max(2, 2 * gauges // count)
    slots = jnp.arange(count * capacity, dtype=jnp.int32)
    same = (owners[:, :, None] == owners[:, None, :]) & (
        jnp.arange(gauges)[None, :] < jnp.arange(gauges)[:, None]
    )
    ranks = jnp.sum(same.astype(jnp.int32), axis=2)
    target = owners * capacity + ranks
    placing = (target[:, :, None] == slots[None, None, :]).astype(f32)
    placed = jnp.einsum(
        "bsg,bgt->bst", values, placing,
        precision=lax.Precision.HIGHEST, preferred_element_type=f32,
    )
    amount = SLAB * sources * capacity
    lanes = -(-amount // LANES) * LANES
    placed = placed.reshape(SLAB, sources, count, capacity).transpose(2, 0, 1, 3)
    placed = jnp.pad(placed.reshape(count, 1, amount), ((0, 0), (0, 0), (0, lanes - amount)))
    arrival, received = pl.pallas_call(
        functools.partial(deliver, count, size),
        out_shape=(jax.ShapeDtypeStruct((rows, width), f32), jax.ShapeDtypeStruct(placed.shape, f32)),
        in_specs=[VMEM, VMEM],
        out_specs=(VMEM, VMEM),
        scratch_shapes=[dma((count,)), dma((count,)), dma((SLAB - 1,)), dma((SLAB,)), dma((2,))],
        compiler_params=pltpu.CompilerParams(collective_id=BLOCKS, has_side_effects=True),
        name="deliver",
    )(arrival, placed)
    received = received[:, 0, :amount].reshape(count // SLAB, SLAB, SLAB, sources, capacity)
    received = jnp.sum(received, axis=1).transpose(2, 0, 1, 3)
    return (arrival, received.reshape(1, sources, count * capacity))


def solution(mesh):
    return jax.shard_map(
        on_device,
        mesh=mesh,
        in_specs=(
            P(("groups", "space"), None),
            P(("groups", "space"), None),
            P("groups", "space", None),
            P("groups"),
            P(("groups", "space")),
            P(("groups", "space"), None),
        ),
        out_specs=(P(("groups", "space"), None), P(("groups", "space"), None, None)),
        check_vma=False,
    )
```
